128 devices in a mesh: segment: 4 (over y_lo, core), hid: 16 (over x, z), wid: 2 (over y_hi).
Axes of the slice: x: 4, y: 4 (y_hi: 2, y_lo: 2; y = y_hi * 2 + y_lo), z: 4, core: 2. Of those that a mesh axis runs over, the one named last changes fastest.
Arguments:
- fwd_input: float32 [128, 5376], P('hid', 'wid'), may hold values from -90 to 90
- saved: float32 [4, 128, 5376], P('segment', 'hid', 'wid'), may hold values from -90 to 90
- cotan: float32 [128, 5376], P('hid', 'wid'), may hold values from -12 to 12
- norm_gain: float32 [4, 5376], P('segment', 'wid'), may hold values from 0.1 to 1.9
- w_gate: bfloat16 [4, 5376, 21504], P('segment', 'wid', 'hid'), may hold values from -0.078125 to 0.078125
- w_up: bfloat16 [4, 5376, 21504], P('segment', 'wid', 'hid'), may hold values from -1 to 1
- w_down: bfloat16 [4, 21504, 5376], P('segment', 'hid', 'wid'), may hold values from -1 to 1
- adapt_a: bfloat16 [4, 5376, 16], P('segment', 'wid'), may hold values from -0.078125 to 0.078125
- adapt_b: bfloat16 [4, 16, 21504], P('segment', None, 'hid'), may hold values from -1.5 to 1.5
Outputs:
- fwd_out: float32 [4, 128, 5376], P('segment', 'hid', 'wid')
- grad_in: float32 [4, 128, 5376], P('segment', 'hid', 'wid')
- grad_a: float32 [4, 5376, 16], P('segment', 'wid')
- grad_b: float32 [4, 16, 21504], P('segment', None, 'hid')
The draws below stay inside these ranges and needn't reach their ends.
All inputs are finite; a program needn't handle non-finite values.
Results may differ from the reference program's by a relative error of at most 0.009.
Values may be sent and summed in bfloat16 or wider, within the bound.
A program may use at most 128 MiB of HBM per device.

```python
import math
import jax
import jax.numpy as jnp
from jax import lax

D = 5376
FF = 21504
RANK = 16
ROWS = 128
SEGMENTS = 4


def row_parts(key, leading):
    first_key, second_key, third_key = jax.random.split(key, 3)
    shape = leading + (ROWS, D)
    base_values = jnp.clip(jax.random.normal(first_key, shape, jnp.float32), -4.0, 4.0)
    row_scales = jnp.exp(jax.random.uniform(second_key, leading + (ROWS, 1), jnp.float32, jnp.log(0.5), jnp.log(5.0)))
    column_ramp = 1.0 + 2.0 * jnp.arange(D, dtype=jnp.float32) / (D - 1)
    column_scales = column_ramp * jnp.exp(jax.random.uniform(third_key, (D,), jnp.float32, -0.35, 0.35))
    return (base_values, row_scales, column_scales)


def scaled_rows(key, leading):
    base_values, row_scales, column_scales = row_parts(key, leading)
    return base_values * row_scales * column_scales


def stream_base(key):
    return row_parts(jax.random.fold_in(key, 12), ())


def draw_fwd_input(key, part):
    return scaled_rows(jax.random.fold_in(key, 11), ())


def draw_saved(key, part):
    base_values, row_scales, column_scales = stream_base(key)
    common = base_values * row_scales * column_scales
    extra = scaled_rows(jax.random.fold_in(key, 14), (SEGMENTS,))
    return 0.7 * common[None] + 0.35 * extra


def draw_cotan(key, part):
    base_values, row_scales, column_scales = stream_base(key)
    noise = jnp.clip(jax.random.normal(jax.random.fold_in(key, 13), (ROWS, D), jnp.float32), -6.0, 6.0)
    return 0.6 * noise + 0.4 * base_values * column_scales


def unit_entries(segment_key, shape):
    return jnp.clip(jax.random.normal(segment_key, shape, jnp.float32), -4.0, 4.0)


def shared_source(key, segment):
    return unit_entries(jax.random.fold_in(jax.random.fold_in(key, 21), segment), (D, FF))


def draw_w_up(key, part):
    segment_ids = jnp.arange(SEGMENTS, dtype=jnp.int32)
    return lax.map(lambda segment: shared_source(key, segment) * (1.0 / math.sqrt(D)), segment_ids).astype(jnp.bfloat16)


def draw_w_down(key, part):
    segment_ids = jnp.arange(SEGMENTS, dtype=jnp.int32)

    def one_segment(segment):
        own = unit_entries(jax.random.fold_in(jax.random.fold_in(key, 22), segment), (FF, D))
        return (0.8 * shared_source(key, segment).T + 0.6 * own) * (1.0 / math.sqrt(FF))
    return lax.map(one_segment, segment_ids).astype(jnp.bfloat16)


def block_levels(key, shape, shards, least, largest):
    level, own = 1.0, jax.random.fold_in(key, 6)
    for axis_at, blocks in shards:
        draws = jnp.exp(jax.random.uniform(jax.random.fold_in(own, axis_at), (blocks,), jnp.float32, least / len(shards), largest / len(shards)))
        level = level * jnp.repeat(draws, shape[axis_at] // blocks).reshape([-1 if axis == axis_at else 1 for axis in range(len(shape))])
    return level


def bell_draw(stream_key, shape, width, most, cuts=(), held_as=jnp.bfloat16):
    array = jax.random.normal(stream_key, shape, jnp.float32) * width
    if len(cuts) > 0:
        array = block_levels(stream_key, shape, cuts, -0.22, 0.18) * array
    return jnp.clip(array, min=-most, max=most).astype(held_as)


def setup_inputs(seed: int = 0) -> dict:
    splits = jax.random.split(jax.random.key(seed), 10)
    return {
        "fwd_input": draw_fwd_input(jax.random.fold_in(splits[9], 71), 0),
        "saved": draw_saved(jax.random.fold_in(splits[9], 71), 0),
        "cotan": draw_cotan(jax.random.fold_in(splits[9], 71), 0),
        "norm_gain": jnp.clip(1.0 + 0.18 * jax.random.normal(splits[3], (SEGMENTS, D), jnp.float32), 0.1, 1.9),
        "w_gate": bell_draw(splits[4], (SEGMENTS, D, FF), D ** -0.5, 0.078125, ((0, 4), (1, 2), (2, 16))),
        "w_up": draw_w_up(jax.random.fold_in(splits[9], 71), 0),
        "w_down": draw_w_down(jax.random.fold_in(splits[9], 71), 0),
        "adapt_a": bell_draw(splits[7], (SEGMENTS, D, RANK), D ** -0.5, 0.078125, ((0, 4), (1, 2))),
        "adapt_b": bell_draw(splits[8], (SEGMENTS, RANK, FF), RANK ** -0.5, 1.5, ((0, 4), (2, 16))),
    }


epsilon = 1e-06
highest = lax.Precision.HIGHEST
ACROSS = (((1,), (1,)), ((), ()))
DOWN_ROWS = (((0,), (0,)), ((), ()))

def gelu_pair(values):
    active, pullback = jax.vjp(lambda inner: jax.nn.gelu(inner, approximate=True), values)
    return (active, pullback(jnp.ones_like(values))[0])

def normalize(inputs, scales):
    inverse = lax.rsqrt(lax.optimization_barrier(jnp.sum(inputs * inputs, axis=1, keepdims=True)) / D + epsilon)
    return (inverse, (inputs * inverse * scales).astype(jnp.bfloat16))

def project(normed, gate_weights, up_weights, adapter_a, adapter_b):
    gate_pre = jnp.dot(normed, gate_weights, preferred_element_type=jnp.float32)
    up_pre = jnp.dot(normed, up_weights, preferred_element_type=jnp.float32)
    low_rank = jnp.dot(normed, adapter_a, preferred_element_type=jnp.float32)
    low_round = low_rank.astype(jnp.bfloat16)
    upward = up_pre + jnp.dot(low_round, adapter_b, preferred_element_type=jnp.float32)
    return (gate_pre, upward, low_round)

def reference(fwd_input, saved, cotan, norm_gain, w_gate, w_up, w_down, adapt_a, adapt_b):
    outputs = []
    current = fwd_input
    for section in range(SEGMENTS):
        inverse, normed = normalize(current, norm_gain[section])
        gate_pre, upward, low_round = project(normed, w_gate[section], w_up[section], adapt_a[section], adapt_b[section])
        hidden = (jax.nn.gelu(gate_pre, approximate=True) * upward).astype(jnp.bfloat16)
        current = current + jnp.dot(hidden, w_down[section], preferred_element_type=jnp.float32)
        outputs.append(current)
    grads_in = [None] * SEGMENTS
    grads_a = [None] * SEGMENTS
    grads_b = [None] * SEGMENTS
    grad_y = cotan
    for section in reversed(range(SEGMENTS)):
        inputs = saved[section]
        scales = norm_gain[section]
        inverse, normed = normalize(inputs, scales)
        gate_pre, upward, low_round = project(normed, w_gate[section], w_up[section], adapt_a[section], adapt_b[section])
        grad_round = grad_y.astype(jnp.bfloat16)
        grad_hidden = lax.dot_general(grad_round, w_down[section], ACROSS, preferred_element_type=jnp.float32)
        active, slopes = gelu_pair(gate_pre)
        grad_gate = (grad_hidden * upward * slopes).astype(jnp.bfloat16)
        grad_up = (grad_hidden * active).astype(jnp.bfloat16)
        grad_low = lax.dot_general(grad_up, adapt_b[section], ACROSS, preferred_element_type=jnp.float32)
        grad_norm = lax.dot_general(grad_gate, w_gate[section], ACROSS, preferred_element_type=jnp.float32)
        grad_norm = grad_norm + lax.dot_general(grad_up, w_up[section], ACROSS, preferred_element_type=jnp.float32)
        grad_norm = grad_norm + jnp.dot(grad_low, adapt_a[section].astype(jnp.float32).T, precision=highest)
        weighted = lax.optimization_barrier(jnp.sum(grad_norm * scales * inputs, axis=1, keepdims=True))
        grad_y = grad_y + inverse * scales * grad_norm - inputs * (inverse * inverse * inverse) * weighted / D
        grads_in[section] = grad_y
        grads_a[section] = jnp.dot(normed.astype(jnp.float32).T, grad_low, precision=highest)
        grads_b[section] = lax.dot_general(low_round, grad_up, DOWN_ROWS, preferred_element_type=jnp.float32)
    return (jnp.stack(outputs), jnp.stack(grads_in), jnp.stack(grads_a), jnp.stack(grads_b))
```

```python
import functools
import math

import jax
import jax.numpy as jnp
from jax import lax
from jax.experimental import pallas as pl
from jax.experimental.pallas import tpu as pltpu
from jax.sharding import PartitionSpec as P

EPSILON = 1e-06
LANES = 128
UNIT_STEP = 512
WIDTH_STEP = 1024
ROOT = math.sqrt(2.0 / math.pi)
CUBE = 0.044715
MESH = pl.DeviceIdType.MESH
ACROSS = (((1,), (1,)), ((), ()))
F32 = jnp.float32
B16 = jnp.bfloat16


def cuts(total, step):
    return [(at, min(step, total - at)) for at in range(0, total, step)]


def up_to(size, step):
    return (size + step - 1) // step * step


def dot(a, b):
    return jnp.dot(a, b, preferred_element_type=F32)


def dot_across(a, b):
    return lax.dot_general(a, b, ACROSS, preferred_element_type=F32)


def two_parts(value):
    high = value.astype(B16).astype(F32)
    return high, value - high


def tail_of(value):
    high, low = two_parts(value)
    lane = lax.broadcasted_iota(jnp.int32, (value.shape[0], LANES), 1)
    return jnp.where(lane == 16, high, jnp.where(lane == 17, low, 0.0))


def kernel(sizes, *refs):
    segments, shards, width, units, rank = sizes
    (fwd_input, saved, cotan, gain, gate_hbm, up_hbm, down_hbm, adapt_a, adapt_b) = refs[:9]
    (fwd_out, grad_in, grad_a, grad_b) = refs[9:13]
    (
        w_gate, w_up, w_down, a_pad, b_pad,
        rows_f, rows_s, rows_b, flat,
        part_f, got_f, part_s, got_s, part_b, got_b,
        low_f, low_got_f, low_s, low_got_s, low_round, low_turned, inverse,
        extra, hidden, d_gate, d_up, slope_term, active_term, inner_term, inner,
        sum_f, back_f, sum_b, back_b,
        thin, thin_got, x_in, g_in, gain_here, gain_next,
        first_message, saved_message, next_message, y_out, g_out,
        sends, recvs, loads,
    ) = refs[13:]
    section = lax.axis_index("segment")
    me = lax.axis_index("hid")
    side = lax.axis_index("wid")
    part = 8
    rows = part * shards
    full = width * 2
    unit_cuts = cuts(units, UNIT_STEP)
    width_cuts = cuts(width, WIDTH_STEP)
    nu, nw = len(unit_cuts), len(width_cuts)
    at = 0
    GF, GS, GB, THIN, XIN, GIN, GAIN = range(7)
    XF = 7
    XS = XF + 1 + 2 * nu
    XB = XS + 1 + 2 * nu
    RF = XB + nu
    RB = RF + nw

    def take(ref, sem):
        pltpu.make_async_copy(ref, ref, sem).wait()

    def weights(index):
        source, target = ((gate_hbm, w_gate), (up_hbm, w_up), (down_hbm, w_down))[index]
        return pltpu.make_async_copy(source.at[0], target, loads.at[index])

    for index in range(3):
        weights(index).start()

    barrier = pltpu.get_barrier_semaphore()

    def greet(who):
        pl.semaphore_signal(barrier, inc=1, device_id=who, device_id_type=MESH)

    def greet_peer(i, carry):
        greet({"hid": lax.rem(me + i, shards)})
        return carry

    lax.fori_loop(1, shards, greet_peer, 0)
    greet({"wid": 1 - side})

    @pl.when(section > 0)
    def _():
        def one(i, carry):
            greet({"segment": section - 1, "hid": lax.rem(me + i, shards)})
            return carry

        lax.fori_loop(0, shards, one, 0)

    @pl.when(section < segments - 1)
    def _():
        def one(i, carry):
            greet({"segment": section + 1, "hid": lax.rem(me + i, shards)})
            return carry

        lax.fori_loop(0, shards, one, 0)

    scales = gain[...]
    gain_here[...] = jnp.broadcast_to(scales, (part, width))

    def message(ref, values, column):
        ref[:, :width] = values.astype(B16)
        ref[:, width:] = tail_of(column).astype(B16)

    saved_rows = saved[0]

    @pl.when(section == 0)
    def _():
        x = fwd_input[...]
        x_in[...] = x
        message(first_message, x * scales, jnp.sum(x * x, axis=1, keepdims=True))

    @pl.when(section == segments - 1)
    def _():
        g = cotan[...]
        g_in[...] = g
        message(first_message, g, jnp.zeros((part, 1), F32))

    message(saved_message, saved_rows * scales, jnp.sum(saved_rows * saved_rows, axis=1, keepdims=True))

    neighbours = jnp.where(section > 0, shards, 0) + jnp.where(section < segments - 1, shards, 0)
    pl.semaphore_wait(barrier, shards + neighbours)

    def spread(source, target, index):
        pltpu.make_async_copy(source, target.at[me], recvs.at[index]).start()

        def one(i, carry):
            pltpu.make_async_remote_copy(
                src_ref=source, dst_ref=target.at[me],
                send_sem=sends.at[index], recv_sem=recvs.at[index],
                device_id={"hid": lax.rem(me + i, shards)}, device_id_type=MESH,
            ).start()
            return carry

        lax.fori_loop(1, shards, one, 0)

    def spread_to(other, source, target, index):
        def one(i, carry):
            pltpu.make_async_remote_copy(
                src_ref=source, dst_ref=target.at[me],
                send_sem=sends.at[index], recv_sem=recvs.at[index],
                device_id={"segment": other, "hid": lax.rem(me + i, shards)}, device_id_type=MESH,
            ).start()
            return carry

        lax.fori_loop(0, shards, one, 0)

    def deliver(source, target, index, columns):
        pltpu.make_async_copy(
            source.at[me, :, columns], target.at[me, :, columns], recvs.at[index]
        ).start()

        def one(i, carry):
            peer = lax.rem(me + i, shards)
            pltpu.make_async_remote_copy(
                src_ref=source.at[peer, :, columns], dst_ref=target.at[me, :, columns],
                send_sem=sends.at[index], recv_sem=recvs.at[index],
                device_id={"hid": peer}, device_id_type=MESH,
            ).start()
            return carry

        lax.fori_loop(1, shards, one, 0)

    def across(source, target, index):
        return pltpu.make_async_remote_copy(
            src_ref=source, dst_ref=target,
            send_sem=sends.at[index], recv_sem=recvs.at[index],
            device_id={"wid": 1 - side}, device_id_type=MESH,
        )

    def onward(other, source, target, index):
        return pltpu.make_async_remote_copy(
            src_ref=source, dst_ref=target,
            send_sem=sends.at[index], recv_sem=recvs.at[index],
            device_id={"segment": other}, device_id_type=MESH,
        )

    @pl.when(section == 0)
    def _():
        spread(first_message, rows_f, GF)

    @pl.when(section == segments - 1)
    def _():
        spread(first_message, rows_b, GB)

    spread(saved_message, rows_s, GS)

    @pl.when(section > 0)
    def _():
        onward(section - 1, gain_here, gain_next, GAIN).start()

    a_pad[...] = jnp.zeros_like(a_pad)
    a_pad[:, :rank] = adapt_a[0]
    b_pad[...] = jnp.zeros_like(b_pad)
    b_pad[:rank, :] = adapt_b[0]
    wide = part_f.shape[2]
    last = units // LANES * LANES
    if last < wide:
        for buffer in (part_f, part_s):
            for j in range(2):
                buffer[j, :, last:] = jnp.zeros((rows, wide - last), B16)
        part_b[:, last:] = jnp.zeros((rows, wide - last), B16)

    def flatten(source):
        def one(i, carry):
            pair = [source[2 * i + j, :, :width].astype(F32) for j in range(2)]
            flat[pl.ds(pl.multiple_of(i * 16, 16), 16), :] = jnp.concatenate(pair, 0).astype(B16)
            return carry

        lax.fori_loop(0, shards // 2, one, 0)

    def cut_of(buffer, start, size):
        return buffer[:, pl.ds(start, up_to(size, LANES))]

    def span(start, size):
        return pl.ds(start, up_to(size, LANES))

    def project(gathered, sem, mine, theirs, low_mine, low_theirs, base):
        take(gathered, recvs.at[sem])
        flatten(gathered)
        tail = gathered[:, :, width:].astype(F32).reshape(rows, LANES)
        low_mine[...] = (dot(flat[...], a_pad[...]) + tail).astype(B16)
        across(low_mine, low_theirs, base).start()
        for c, (start, size) in enumerate(unit_cuts):
            for j, matrix in enumerate((w_gate, w_up)):
                mine[j, :, start : start + size] = dot(
                    flat[...], matrix[:, start : start + size]
                ).astype(B16)
                across(
                    mine.at[j, :, span(start, size)],
                    theirs.at[j, :, span(start, size)],
                    base + 1 + 2 * c + j,
                ).start()

    def join_low(low_mine, low_theirs, base):
        take(low_theirs, recvs.at[base])
        low = low_mine[...].astype(F32) + low_theirs[...].astype(F32)
        squares = low[:, 16:17] + low[:, 17:18]
        inv = lax.rsqrt(squares / full + EPSILON)
        inverse[...] = jnp.broadcast_to(inv, (rows, LANES))
        lane = lax.broadcasted_iota(jnp.int32, (rows, LANES), 1)
        low = jnp.where(lane < rank, low * inv, 0.0)
        low_round[...] = low.astype(B16)
        return low

    def each_block(work):
        def one(i, carry):
            work(pl.ds(pl.multiple_of(i * 16, 16), 16))
            return carry

        lax.fori_loop(0, rows // 16, one, 0)

    def join_units(mine, theirs, base, work):
        for c, (start, size) in enumerate(unit_cuts):
            for j in range(2):
                take(theirs.at[j, :, span(start, size)], recvs.at[base + 1 + 2 * c + j])
            extra[:, :size] = dot(low_round[...], b_pad[:, start : start + size])
            here = slice(start, start + size)

            def block(at_rows):
                inv = inverse[at_rows, :1]
                gate = mine[0, at_rows, here].astype(F32) + theirs[0, at_rows, here].astype(F32)
                up = mine[1, at_rows, here].astype(F32) + theirs[1, at_rows, here].astype(F32)
                work(at_rows, here, gate * inv, up * inv + extra[at_rows, :size])

            each_block(block)

    def total(received, index, take_columns):
        for c, (start, size) in enumerate(width_cuts):
            more = take_columns(c)
            take(received.at[:, :, pl.ds(start, size + more)], recvs.at[index + c])
            value = received[0, :, start : start + size + more].astype(F32)
            for k in range(1, shards):
                value = value + received[k, :, start : start + size + more].astype(F32)
            yield start, size, value

    def forward():
        project(rows_f, GF, part_f, got_f, low_f, low_got_f, XF)
        join_low(low_f, low_got_f, XF)

        def work(at_rows, here, gate, up):
            bend = jnp.tanh(ROOT * (gate + CUBE * gate * gate * gate))
            hidden[at_rows, here] = (0.5 * gate * (1.0 + bend) * up).astype(B16)

        join_units(part_f, got_f, XF, work)
        for c, (start, size) in enumerate(width_cuts):
            value = dot(hidden[...], w_down[:, start : start + size])
            sum_f[:, :, start : start + size] = value.reshape(shards, part, size).astype(B16)
            deliver(sum_f, back_f, RF + c, pl.ds(start, size))

        @pl.when(section > 0)
        def _():
            take(x_in, recvs.at[XIN])

        squares = jnp.zeros((part, 1), F32)

        @pl.when(section < segments - 1)
        def _():
            take(gain_next, recvs.at[GAIN])

        for start, size, value in total(back_f, RF, lambda c: 0):
            y = x_in[:, start : start + size] + value
            y_out[:, start : start + size] = y
            squares = squares + jnp.sum(y * y, axis=1, keepdims=True)

        @pl.when(section < segments - 1)
        def _():
            message(next_message.at[0], y_out[...] * gain_next[...], squares)
            spread_to(section + 1, next_message.at[0], rows_f, GF)
            onward(section + 1, y_out, x_in, XIN).start()

        fwd_out[0] = y_out[...]

    def recompute():
        project(rows_s, GS, part_s, got_s, low_s, low_got_s, XS)
        low = join_low(low_s, low_got_s, XS)
        low_turned[...] = low.T.astype(B16)

        def work(at_rows, here, gate, up):
            bend = jnp.tanh(ROOT * (gate + CUBE * gate * gate * gate))
            active = 0.5 * gate * (1.0 + bend)
            slope = 0.5 * (1.0 + bend) + 0.5 * gate * (1.0 - bend * bend) * (
                ROOT * (1.0 + 3.0 * CUBE * gate * gate)
            )
            steep = up * slope
            slope_term[at_rows, here] = steep
            active_term[at_rows, here] = active
            inner_term[at_rows, here] = steep * gate + active * up

        join_units(part_s, got_s, XS, work)
        inverse_saved = inner.at[1]
        inverse_saved[...] = inverse[...]

    def backward():
        take(rows_b, recvs.at[GB])
        flatten(rows_b)
        for c, (start, size) in enumerate(unit_cuts):
            part_b[:, start : start + size] = dot_across(
                flat[...], w_down[start : start + size, :]
            ).astype(B16)
            across(
                part_b.at[:, span(start, size)], got_b.at[:, span(start, size)], XB + c
            ).start()
        inner[0] = jnp.zeros((rows, LANES), F32)
        for c, (start, size) in enumerate(unit_cuts):
            take(got_b.at[:, span(start, size)], recvs.at[XB + c])
            here = slice(start, start + size)

            def block(at_rows):
                d_hid = part_b[at_rows, here].astype(F32) + got_b[at_rows, here].astype(F32)
                d_gate[at_rows, here] = (d_hid * slope_term[at_rows, here]).astype(B16)
                d_up[at_rows, here] = (d_hid * active_term[at_rows, here]).astype(B16)
                inner[0, at_rows, :] += jnp.broadcast_to(
                    jnp.sum(d_hid * inner_term[at_rows, here], axis=1, keepdims=True), (16, LANES)
                )

            each_block(block)
        d_low = dot_across(d_up[...], b_pad[...])
        d_low_round = d_low.astype(B16)
        thin_mine = (d_low * inner[1]).T[:rank]
        thin[...] = thin_mine

        def one(i, carry):
            pltpu.make_async_remote_copy(
                src_ref=thin, dst_ref=thin_got.at[me],
                send_sem=sends.at[THIN], recv_sem=recvs.at[THIN],
                device_id={"hid": lax.rem(me + i, shards)}, device_id_type=MESH,
            ).start()
            return carry

        tail = tail_of(inner[0][:, :1])
        sum_b[:, :, width:] = tail.reshape(shards, part, LANES).astype(B16)
        for c, (start, size) in enumerate(width_cuts):
            value = dot_across(d_gate[...], w_gate[start : start + size, :])
            value = value + dot_across(d_up[...], w_up[start : start + size, :])
            value = value + dot_across(d_low_round, a_pad[start : start + size, :])
            sum_b[:, :, start : start + size] = value.reshape(shards, part, size).astype(B16)
            more = LANES if c == nw - 1 else 0
            deliver(sum_b, back_b, RB + c, pl.ds(start, size + more))
        pltpu.make_async_copy(thin, thin_got.at[me], recvs.at[THIN]).start()
        lax.fori_loop(1, shards, one, 0)
        grad_b[0] = dot(low_turned[...], d_up[...])[:rank]

        @pl.when(section < segments - 1)
        def _():
            take(g_in, recvs.at[GIN])

        inv = inner[1, pl.ds(pl.multiple_of(me * part, part), part), :][:, :1]
        parts = list(total(back_b, RB, lambda c: LANES if c == nw - 1 else 0))
        start, size, value = parts[-1]
        weight = value[:, size + 16 : size + 17] + value[:, size + 17 : size + 18]
        weight = inv * inv * weight / full
        for start, size, value in parts:
            here = slice(start, start + size)
            g_out[:, here] = (
                g_in[:, here]
                + inv * gain_here[:, here] * value[:, :size]
                - saved[0, :, here] * weight
            )

        @pl.when(section > 0)
        def _():
            message(next_message.at[1], g_out[...], jnp.zeros((part, 1), F32))
            spread_to(section - 1, next_message.at[1], rows_b, GB)
            onward(section - 1, g_out, g_in, GIN).start()

        grad_in[0] = g_out[...]
        take(thin_got, recvs.at[THIN])
        low_sum = thin_got[0]
        for k in range(1, shards):
            low_sum = low_sum + thin_got[k]
        high, low = two_parts(low_sum)
        flatten(rows_s)
        turned = dot(high.astype(B16), flat[...]) + dot(low.astype(B16), flat[...])
        for at_lane in range(0, width, LANES):
            block = jnp.concatenate(
                [turned[:, at_lane : at_lane + LANES], jnp.zeros((LANES - rank, LANES), F32)], 0
            )
            grad_a[0, at_lane : at_lane + LANES, :] = block.T[:, :rank]

    for index in range(3):
        weights(index).wait()

    def moment(now, carry):
        pl.when(section == now)(forward)
        pl.when(now == 0)(recompute)
        pl.when(section == segments - 1 - now)(backward)
        return carry

    lax.fori_loop(0, segments, moment, 0)

    def sent(ref, index):
        take(ref, sends.at[index])

    others = pl.ds(0, shards - 1)

    @pl.when(section == 0)
    def _():
        sent(rows_f.at[others], GF)
        sent(rows_f, GF)

    @pl.when(jnp.logical_and(section > 0, section < segments - 1))
    def _():
        sent(rows_f, GF)
        sent(rows_b, GB)

    @pl.when(section == segments - 1)
    def _():
        sent(rows_b.at[others], GB)
        sent(rows_b, GB)

    @pl.when(section > 0)
    def _():
        sent(gain_here, GAIN)
        sent(g_out, GIN)

    @pl.when(section < segments - 1)
    def _():
        sent(y_out, XIN)

    sent(rows_s.at[others], GS)
    sent(thin_got.at[others], THIN)
    for base, low_mine, mine in ((XF, low_f, part_f), (XS, low_s, part_s)):
        sent(low_mine, base)
        for c, (start, size) in enumerate(unit_cuts):
            for j in range(2):
                sent(mine.at[j, :, span(start, size)], base + 1 + 2 * c + j)
    for c, (start, size) in enumerate(unit_cuts):
        sent(part_b.at[:, span(start, size)], XB + c)
    for c, (start, size) in enumerate(width_cuts):
        more = LANES if c == nw - 1 else 0
        sent(sum_f.at[others, :, pl.ds(start, size)], RF + c)
        sent(sum_b.at[others, :, pl.ds(start, size + more)], RB + c)


def body(*args):
    fwd_input, saved, cotan, norm_gain, w_gate, w_up, w_down, adapt_a, adapt_b = args
    segments = lax.axis_size("segment")
    shards = lax.axis_size("hid")
    part, width = fwd_input.shape
    units = w_gate.shape[2]
    rank = adapt_a.shape[2]
    rows = part * shards
    wide = up_to(units, LANES)
    long = width + LANES
    nu, nw = len(cuts(units, UNIT_STEP)), len(cuts(width, WIDTH_STEP))
    groups = 9 + 4 * nu + nu + 2 * nw
    vmem = pltpu.VMEM
    gathered = vmem((shards, part, long), B16)
    pair = vmem((2, rows, wide), B16)
    single = vmem((rows, wide), B16)
    square = vmem((rows, LANES), B16)
    term = vmem((rows, units), F32)
    eight = vmem((part, width), F32)
    line = vmem((part, long), B16)
    scratch = [
        vmem((width, units), B16), vmem((width, units), B16), vmem((units, width), B16),
        vmem((width, LANES), B16), vmem((LANES, units), B16),
        gathered, gathered, gathered, vmem((rows, width), B16),
        pair, pair, pair, pair, single, single,
        square, square, square, square, square, vmem((LANES, rows), B16), vmem((rows, LANES), F32),
        vmem((rows, min(UNIT_STEP, units)), F32),
        vmem((rows, units), B16), vmem((rows, units), B16), vmem((rows, units), B16),
        term, term, term, vmem((2, rows, LANES), F32),
        gathered, gathered, gathered, gathered,
        vmem((rank, rows), F32), vmem((shards, rank, rows), F32),
        eight, eight, eight, eight,
        line, line, vmem((2, part, long), B16), eight, eight,
        pltpu.SemaphoreType.DMA((groups,)), pltpu.SemaphoreType.DMA((groups,)),
        pltpu.SemaphoreType.DMA((3,)),
    ]
    whole = pl.BlockSpec(memory_space=pltpu.VMEM)
    away = pl.BlockSpec(memory_space=pl.ANY)
    return pl.pallas_call(
        functools.partial(kernel, (segments, shards, width, units, rank)),
        out_shape=(
            jax.ShapeDtypeStruct((1, part, width), F32),
            jax.ShapeDtypeStruct((1, part, width), F32),
            jax.ShapeDtypeStruct((1, width, rank), F32),
            jax.ShapeDtypeStruct((1, rank, units), F32),
        ),
        in_specs=[whole] * 4 + [away] * 3 + [whole] * 2,
        out_specs=(whole,) * 4,
        scratch_shapes=scratch,
        compiler_params=pltpu.CompilerParams(
            collective_id=0, has_side_effects=True, vmem_limit_bytes=56 * 1024 * 1024
        ),
    )(*args)


def solution(mesh):
    placed = (
        P("hid", "wid"),
        P("segment", "hid", "wid"),
        P("hid", "wid"),
        P("segment", "wid"),
        P("segment", "wid", "hid"),
        P("segment", "wid", "hid"),
        P("segment", "hid", "wid"),
        P("segment", "wid", None),
        P("segment", None, "hid"),
    )
    return jax.shard_map(
        body,
        mesh=mesh,
        in_specs=placed,
        out_specs=(
            P("segment", "hid", "wid"),
            P("segment", "hid", "wid"),
            P("segment", "wid", None),
            P("segment", None, "hid"),
        ),
        check_vma=False,
    )
```

```python
import functools
import math

import jax
import jax.numpy as jnp
from jax import lax
from jax.experimental import pallas as pl
from jax.experimental.pallas import tpu as pltpu
from jax.sharding import PartitionSpec as P

EPSILON = 1e-06
LANES = 128
UNIT_STEP = 512
WIDTH_STEP = 768
ROOT = math.sqrt(2.0 / math.pi)
CUBE = 0.044715
MESH = pl.DeviceIdType.MESH
ACROSS = (((1,), (1,)), ((), ()))
F32 = jnp.float32
B16 = jnp.bfloat16


def cuts(total, step):
    return [(at, min(step, total - at)) for at in range(0, total, step)]


def up_to(size, step):
    return (size + step - 1) // step * step


def dot(a, b):
    return jnp.dot(a, b, preferred_element_type=F32)


def dot_across(a, b):
    return lax.dot_general(a, b, ACROSS, preferred_element_type=F32)


def two_parts(value):
    high = value.astype(B16).astype(F32)
    return high, value - high


def tail_of(value):
    high, low = two_parts(value)
    lane = lax.broadcasted_iota(jnp.int32, (value.shape[0], LANES), 1)
    return jnp.where(lane == 16, high, jnp.where(lane == 17, low, 0.0))


def turn_rows(value):
    return jnp.concatenate([value[..., 4:, :], value[..., :4, :]], axis=-2)


def swap(first, second):
    row = lax.broadcasted_iota(jnp.int32, first.shape, first.ndim - 2)
    upper = jnp.where(row < 4, first, turn_rows(second))
    lower = jnp.where(row < 4, turn_rows(first), second)
    return upper, lower


def kernel(sizes, *refs):
    segments, shards, width, units, rank = sizes
    (fwd_input, saved, cotan, gain, gate_hbm, up_hbm, down_hbm, adapt_a, adapt_b) = refs[:9]
    (fwd_out, grad_in, grad_a, grad_b) = refs[9:13]
    (
        w_gate, w_up, w_down, a_pad, b_pad,
        rows_f, rows_s, rows_b, flat,
        part_f, got_f, part_s, got_s, part_b, got_b,
        low_f, low_got_f, low_s, low_got_s, low_round, low_turned, inverse,
        tails, extra, hidden, d_gate, d_up, slope_term, active_term, inner_term, inner,
        sum_f, back_f, sum_b, back_b,
        thin, thin_got, x_in, g_in, x_saved, gain_here, gain_next,
        first_message, saved_message, next_message, y_out, g_out,
        sends, recvs, loads, turn,
    ) = refs[13:]
    section = lax.axis_index("segment")
    me = lax.axis_index("hid")
    side = lax.axis_index("wid")
    part = 8
    rows = part * shards
    full = width * 2
    unit_cuts = cuts(units, UNIT_STEP)
    fold = (width + LANES) // 2
    rest = width - fold
    width_cuts = cuts(fold, WIDTH_STEP)
    nu, nw = len(unit_cuts), len(width_cuts)
    batch_rows = rows // 2
    GF, GS, GB, THIN, XIN, GIN, GAIN = 0, 2, 4, 6, 7, 9, 11
    XF = 12
    XS = XF + 2 * (1 + 2 * nu)
    XB = XS + 2 * (1 + 2 * nu)
    RF = XB + 2 * nu
    RB = RF + 2 * nw

    def take(ref, sem):
        pltpu.make_async_copy(ref, ref, sem).wait()

    def weights(index):
        source, target = ((gate_hbm, w_gate), (up_hbm, w_up), (down_hbm, w_down))[index]
        return pltpu.make_async_copy(source.at[0], target, loads.at[index])

    for index in range(3):
        weights(index).start()

    barrier = pltpu.get_barrier_semaphore()

    def greet(who):
        pl.semaphore_signal(barrier, inc=1, device_id=who, device_id_type=MESH)

    def greet_peer(i, carry):
        greet({"hid": lax.rem(me + i, shards)})
        return carry

    lax.fori_loop(1, shards, greet_peer, 0)
    greet({"wid": 1 - side})

    @pl.when(section > 0)
    def _():
        def one(i, carry):
            greet({"segment": section - 1, "hid": lax.rem(me + i, shards)})
            return carry

        lax.fori_loop(0, shards, one, 0)

    @pl.when(section < segments - 1)
    def _():
        def one(i, carry):
            greet({"segment": section + 1, "hid": lax.rem(me + i, shards)})
            return carry

        lax.fori_loop(0, shards, one, 0)

    row8 = lax.broadcasted_iota(jnp.int32, (8, LANES), 0)

    def folded(values, tail):
        return swap(values[:, :fold], jnp.concatenate([values[:, fold:], tail], 1))

    def rounded(ref, values, tail):
        for batch, value in enumerate(folded(values, tail)):
            ref[batch] = value.astype(B16)

    nothing = jnp.zeros((part, LANES), F32)
    scales = jnp.broadcast_to(gain[...], (part, width))
    gain_here[...] = folded(scales, nothing)[0]
    saved_rows = saved[0]
    for batch, value in enumerate(folded(saved_rows, nothing)):
        x_saved[batch] = value

    def message(ref, x):
        rounded(ref, x * scales, tail_of(jnp.sum(x * x, axis=1, keepdims=True)))

    @pl.when(section == 0)
    def _():
        x = fwd_input[...]
        for batch, value in enumerate(folded(x, nothing)):
            x_in[batch] = value
        message(first_message, x)

    @pl.when(section == segments - 1)
    def _():
        g = cotan[...]
        for batch, value in enumerate(folded(g, nothing)):
            g_in[batch] = value
        rounded(first_message, g, nothing)

    message(saved_message, saved_rows)

    neighbours = jnp.where(section > 0, shards, 0) + jnp.where(section < segments - 1, shards, 0)
    pl.semaphore_wait(barrier, shards + neighbours)

    def spread(source, target, index, batch):
        pltpu.make_async_copy(
            source.at[batch], target.at[batch, me], recvs.at[index + batch]
        ).start()

        def one(i, carry):
            pltpu.make_async_remote_copy(
                src_ref=source.at[batch], dst_ref=target.at[batch, me],
                send_sem=sends.at[index + batch], recv_sem=recvs.at[index + batch],
                device_id={"hid": lax.rem(me + i, shards)}, device_id_type=MESH,
            ).start()
            return carry

        lax.fori_loop(1, shards, one, 0)

    def spread_both(source, target, index):
        for batch in range(2):
            spread(source, target, index, batch)

    def spread_to(other, source, target, index, batch):
        def one(i, carry):
            pltpu.make_async_remote_copy(
                src_ref=source.at[batch], dst_ref=target.at[batch, me],
                send_sem=sends.at[index + batch], recv_sem=recvs.at[index + batch],
                device_id={"segment": other, "hid": lax.rem(me + i, shards)}, device_id_type=MESH,
            ).start()
            return carry

        lax.fori_loop(0, shards, one, 0)

    def deliver(source, target, index, batch, columns):
        pltpu.make_async_copy(
            source.at[batch, me, :, columns], target.at[batch, me, :, columns], recvs.at[index]
        ).start()

        def one(i, carry):
            peer = lax.rem(me + i, shards)
            pltpu.make_async_remote_copy(
                src_ref=source.at[batch, peer, :, columns],
                dst_ref=target.at[batch, me, :, columns],
                send_sem=sends.at[index], recv_sem=recvs.at[index],
                device_id={"hid": peer}, device_id_type=MESH,
            ).start()
            return carry

        lax.fori_loop(1, shards, one, 0)

    def across(source, target, index):
        return pltpu.make_async_remote_copy(
            src_ref=source, dst_ref=target,
            send_sem=sends.at[index], recv_sem=recvs.at[index],
            device_id={"wid": 1 - side}, device_id_type=MESH,
        )

    def onward(other, source, target, index):
        return pltpu.make_async_remote_copy(
            src_ref=source, dst_ref=target,
            send_sem=sends.at[index], recv_sem=recvs.at[index],
            device_id={"segment": other}, device_id_type=MESH,
        )

    @pl.when(section == 0)
    def _():
        spread(first_message, rows_f, GF, 0)

    @pl.when(section == segments - 1)
    def _():
        spread_both(saved_message, rows_s, GS)
        spread_both(first_message, rows_b, GB)

    @pl.when(section > 0)
    def _():
        onward(section - 1, gain_here, gain_next, GAIN).start()

    a_pad[...] = jnp.zeros_like(a_pad)
    a_pad[:rank, :] = adapt_a[0]
    b_pad[...] = jnp.zeros_like(b_pad)
    b_pad[:rank, :] = adapt_b[0]
    wide = part_f.shape[2]
    last = units // LANES * LANES
    if last < wide:
        for buffer in (part_f, part_s):
            for j in range(2):
                buffer[j, :, last:] = jnp.zeros((rows, wide - last), B16)
        part_b[:, last:] = jnp.zeros((rows, wide - last), B16)

    def rows_of(batch):
        return slice(batch * batch_rows, (batch + 1) * batch_rows)

    @pl.when(section == 0)
    def _():
        spread(first_message, rows_f, GF, 1)

    def flatten(source, batch):
        def one(i, carry):
            lefts, rights = [], []
            for j in range(2):
                pair = [source[batch, 4 * i + 2 * j + k].astype(F32) for k in range(2)]
                left, right = swap(pair[0], pair[1])
                lefts.append(left)
                rights.append(right)
            at_rows = pl.ds(pl.multiple_of(batch * batch_rows + i * 16, 16), 16)
            right = jnp.concatenate(rights, 0)
            flat[at_rows, :fold] = jnp.concatenate(lefts, 0).astype(B16)
            flat[at_rows, fold:] = right[:, :rest].astype(B16)
            tails[at_rows, :] = right[:, rest:]
            return carry

        lax.fori_loop(0, shards // 4, one, 0)

    def span(start, size):
        return pl.ds(start, up_to(size, LANES))

    def arrived(gathered, index, batch):
        take(gathered.at[batch], recvs.at[index + batch])
        flatten(gathered, batch)

    def project(gathered, index, mine, theirs, low_mine, low_theirs, base, batches):
        step = 1 + 2 * nu
        here = slice(batches[0] * batch_rows, (batches[-1] + 1) * batch_rows)
        for batch in batches:
            arrived(gathered, index, batch)
        low_mine[here, :] = (dot_across(flat[here, :], a_pad[...]) + tails[here, :]).astype(B16)
        for batch in batches:
            ours = rows_of(batch)
            across(low_mine.at[ours], low_theirs.at[ours], base + batch * step).start()
        for c, (start, size) in enumerate(unit_cuts):
            for j, matrix in enumerate((w_gate, w_up)):
                mine[j, here, start : start + size] = dot_across(
                    flat[here, :], matrix[start : start + size, :]
                ).astype(B16)
                for batch in batches:
                    ours = rows_of(batch)
                    across(
                        mine.at[j, ours, span(start, size)],
                        theirs.at[j, ours, span(start, size)],
                        base + batch * step + 1 + 2 * c + j,
                    ).start()

    def join_low(low_mine, low_theirs, base, batch):
        base = base + batch * (1 + 2 * nu)
        here = rows_of(batch)
        take(low_theirs.at[here], recvs.at[base])
        low = low_mine[here, :].astype(F32) + low_theirs[here, :].astype(F32)
        squares = low[:, 16:17] + low[:, 17:18]
        inv = lax.rsqrt(squares / full + EPSILON)
        inverse[here, :] = jnp.broadcast_to(inv, (batch_rows, LANES))
        lane = lax.broadcasted_iota(jnp.int32, (batch_rows, LANES), 1)
        low_round[here, :] = jnp.where(lane < rank, low * inv, 0.0).astype(B16)

    def each_block(work, batch):
        def one(i, carry):
            work(pl.ds(pl.multiple_of(batch * batch_rows + i * 16, 16), 16), i)
            return carry

        lax.fori_loop(0, batch_rows // 16, one, 0)

    def join_units(mine, theirs, base, work, batch):
        base = base + batch * (1 + 2 * nu)
        rows_here = rows_of(batch)
        for c, (start, size) in enumerate(unit_cuts):
            for j in range(2):
                take(theirs.at[j, rows_here, span(start, size)], recvs.at[base + 1 + 2 * c + j])
            extra[:, :size] = dot(low_round[rows_here, :], b_pad[:, start : start + size])
            here = slice(start, start + size)

            def block(at_rows, i):
                inv = inverse[at_rows, :1]
                gate = mine[0, at_rows, here].astype(F32) + theirs[0, at_rows, here].astype(F32)
                up = mine[1, at_rows, here].astype(F32) + theirs[1, at_rows, here].astype(F32)
                added = extra[pl.ds(pl.multiple_of(i * 16, 16), 16), :size]
                work(at_rows, here, gate * inv, up * inv + added)

            each_block(block, batch)

    def pack(target, batch, start, size, left, right):
        shape = (shards // 2, 8, size)
        even, odd = swap(left.reshape(shape), right.reshape(shape))
        for i in range(shards // 2):
            target[batch, 2 * i, :, start : start + size] = even[i].astype(B16)
            target[batch, 2 * i + 1, :, start : start + size] = odd[i].astype(B16)

    def total(received, index, batch):
        parts = []
        for c, (start, size) in enumerate(width_cuts):
            take(received.at[batch, :, :, pl.ds(start, size)], recvs.at[index + batch * nw + c])
            value = received[batch, 0, :, start : start + size].astype(F32)
            for k in range(1, shards):
                value = value + received[batch, k, :, start : start + size].astype(F32)
            parts.append(value)
        return jnp.concatenate(parts, 1)

    def send_on(other, values, tail, batch, slot, target, index):
        message_ref = next_message.at[slot]
        message_ref[batch, :, :rest] = values[:, :rest].astype(B16)
        message_ref[batch, :, rest:] = jnp.where(row8 < 4, values[:, rest:], tail).astype(B16)
        spread_to(other, message_ref, target, index, batch)

    def unfold(target, blocks):
        left, right = swap(blocks[0], blocks[1])
        target[0, :, :fold] = left
        target[0, :, fold:] = right[:, :rest]

    def forward():
        for batch in range(2):
            project(rows_f, GF, part_f, got_f, low_f, low_got_f, XF, (batch,))

        @pl.when(section == 1)
        def _():
            spread_both(saved_message, rows_s, GS)

        def work(at_rows, here, gate, up):
            bend = jnp.tanh(ROOT * (gate + CUBE * gate * gate * gate))
            hidden[at_rows, here] = (0.5 * gate * (1.0 + bend) * up).astype(B16)

        for batch in range(2):
            join_low(low_f, low_got_f, XF, batch)
            join_units(part_f, got_f, XF, work, batch)
            h = hidden[rows_of(batch), :]
            for c, (start, size) in enumerate(width_cuts):
                left = dot(h, w_down[:, start : start + size])
                real = min(size, rest - start)
                right = dot(h, w_down[:, fold + start : fold + start + real])
                if real < size:
                    right = jnp.concatenate([right, jnp.zeros((batch_rows, size - real), F32)], 1)
                pack(sum_f, batch, start, size, left, right)
                deliver(sum_f, back_f, RF + batch * nw + c, batch, pl.ds(start, size))

        @pl.when(section < segments - 1)
        def _():
            take(gain_next, recvs.at[GAIN])

        for batch in range(2):

            @pl.when(section > 0)
            def _():
                take(x_in.at[batch], recvs.at[XIN + batch])

            value = total(back_f, RF, batch)
            bottom = jnp.where(row8 < 4, value[:, rest:], 0.0)
            y = x_in[batch] + jnp.concatenate([value[:, :rest], bottom], 1)
            y_out[batch] = y

            @pl.when(section < segments - 1)
            def _():
                squares = jnp.sum(y * y, axis=1, keepdims=True)
                tail = tail_of(squares + turn_rows(squares))
                send_on(section + 1, y * gain_next[...], tail, batch, 0, rows_f, GF)
                onward(section + 1, y_out.at[batch], x_in.at[batch], XIN + batch).start()

        unfold(fwd_out, (y_out[0], y_out[1]))

    def recompute():
        @pl.when(jnp.logical_or(section == 0, section == 2))
        def _():
            pl.semaphore_wait(turn, 1)
            spread_both(saved_message, rows_s, GS)

        project(rows_s, GS, part_s, got_s, low_s, low_got_s, XS, (0, 1))

        @pl.when(section == 1)
        def _():
            pl.semaphore_signal(turn, inc=1, device_id={"segment": 0}, device_id_type=MESH)

    def join_saved():
        def work(at_rows, here, gate, up):
            bend = jnp.tanh(ROOT * (gate + CUBE * gate * gate * gate))
            active = 0.5 * gate * (1.0 + bend)
            slope = 0.5 * (1.0 + bend) + 0.5 * gate * (1.0 - bend * bend) * (
                ROOT * (1.0 + 3.0 * CUBE * gate * gate)
            )
            steep = up * slope
            slope_term[at_rows, here] = steep
            active_term[at_rows, here] = active
            inner_term[at_rows, here] = steep * gate + active * up

        for batch in range(2):
            join_low(low_s, low_got_s, XS, batch)
            join_units(part_s, got_s, XS, work, batch)
        inner[1] = inverse[...]
        low_turned[...] = low_round[...].astype(F32).T.astype(B16)

    def backward():
        for batch in range(2):
            arrived(rows_b, GB, batch)
            at_rows = rows_of(batch)
            for c, (start, size) in enumerate(unit_cuts):
                part_b[at_rows, start : start + size] = dot_across(
                    flat[at_rows, :], w_down[start : start + size, :]
                ).astype(B16)
                across(
                    part_b.at[at_rows, span(start, size)],
                    got_b.at[at_rows, span(start, size)],
                    XB + batch * nu + c,
                ).start()

        @pl.when(section == segments - 1)
        def _():
            pl.semaphore_signal(turn, inc=1, device_id={"segment": 2}, device_id_type=MESH)

        join_saved()
        inner[0] = jnp.zeros((rows, LANES), F32)
        for batch in range(2):
            ours = rows_of(batch)
            for c, (start, size) in enumerate(unit_cuts):
                take(got_b.at[ours, span(start, size)], recvs.at[XB + batch * nu + c])
                here = slice(start, start + size)

                def block(at_rows, i):
                    d_hid = part_b[at_rows, here].astype(F32) + got_b[at_rows, here].astype(F32)
                    d_gate[at_rows, here] = (d_hid * slope_term[at_rows, here]).astype(B16)
                    d_up[at_rows, here] = (d_hid * active_term[at_rows, here]).astype(B16)
                    inner[0, at_rows, :] += jnp.broadcast_to(
                        jnp.sum(d_hid * inner_term[at_rows, here], axis=1, keepdims=True),
                        (16, LANES),
                    )

                each_block(block, batch)
            d_low_round = dot_across(d_up[ours, :], b_pad[...]).astype(B16)
            tail = tail_of(inner[0, ours, :1])

            def product(start, size):
                here = slice(start, start + size)
                value = dot(d_gate[ours, :], w_gate[:, here])
                value = value + dot(d_up[ours, :], w_up[:, here])
                return value + dot(d_low_round, a_pad[:, here])

            for c, (start, size) in enumerate(width_cuts):
                left = product(start, size)
                real = min(size, rest - start)
                right = product(fold + start, real)
                if real < size:
                    right = jnp.concatenate([right, tail], 1)
                pack(sum_b, batch, start, size, left, right)
                deliver(sum_b, back_b, RB + batch * nw + c, batch, pl.ds(start, size))
        d_low = dot_across(d_up[...], b_pad[...])
        thin[...] = (d_low * inner[1]).T[:rank]

        def one(i, carry):
            pltpu.make_async_remote_copy(
                src_ref=thin, dst_ref=thin_got.at[me],
                send_sem=sends.at[THIN], recv_sem=recvs.at[THIN],
                device_id={"hid": lax.rem(me + i, shards)}, device_id_type=MESH,
            ).start()
            return carry

        pltpu.make_async_copy(thin, thin_got.at[me], recvs.at[THIN]).start()
        lax.fori_loop(1, shards, one, 0)
        grad_b[0] = dot(low_turned[...], d_up[...])[:rank]

        for batch in range(2):

            @pl.when(section < segments - 1)
            def _():
                take(g_in.at[batch], recvs.at[GIN + batch])

            at_row = pl.multiple_of(batch * batch_rows + me // 2 * 8, 8)
            inv = inner[1, pl.ds(at_row, 8), :]
            upper = jnp.where(lax.rem(me, 2) == 0, 0, 4)
            inv = jnp.where(row8 // 4 * 4 == upper, inv, turn_rows(inv))[:, :1]
            value = total(back_b, RB, batch)
            weight = value[:, rest + 16 : rest + 17] + value[:, rest + 17 : rest + 18]
            weight = jnp.where(row8 < 4, turn_rows(weight), weight)[:, :1]
            weight = inv * inv * weight / full
            g = g_in[batch] + inv * gain_here[...] * value - x_saved[batch] * weight
            g_out[batch] = g

            @pl.when(section > 0)
            def _():
                send_on(section - 1, g, nothing, batch, 1, rows_b, GB)
                onward(section - 1, g_out.at[batch], g_in.at[batch], GIN + batch).start()

        unfold(grad_in, (g_out[0], g_out[1]))
        take(thin_got, recvs.at[THIN])
        low_sum = thin_got[0]
        for k in range(1, shards):
            low_sum = low_sum + thin_got[k]
        high, low = two_parts(low_sum)
        for batch in range(2):
            flatten(rows_s, batch)
        grad_a[0] = dot(high.astype(B16), flat[...]) + dot(low.astype(B16), flat[...])

    for index in range(3):
        weights(index).wait()

    def moment(now, carry):
        pl.when(section == now)(forward)
        pl.when(now == jnp.where(section == 1, 1, 0))(recompute)
        pl.when(section == segments - 1 - now)(backward)
        return carry

    lax.fori_loop(0, segments, moment, 0)

    def sent(ref, index):
        take(ref, sends.at[index])

    others = pl.ds(0, shards - 1)
    for batch in range(2):

        @pl.when(section < segments - 1)
        def _():
            sent(rows_f.at[batch], GF + batch)
            sent(y_out.at[batch], XIN + batch)

        @pl.when(section > 0)
        def _():
            sent(rows_b.at[batch], GB + batch)
            sent(g_out.at[batch], GIN + batch)

        @pl.when(section == 0)
        def _():
            sent(rows_f.at[batch, others], GF + batch)

        @pl.when(section == segments - 1)
        def _():
            sent(rows_b.at[batch, others], GB + batch)

        sent(rows_s.at[batch, others], GS + batch)

    @pl.when(section > 0)
    def _():
        sent(gain_here, GAIN)

    sent(thin_got.at[others], THIN)
    for batch in range(2):
        here = rows_of(batch)
        for first, low_mine, mine in ((XF, low_f, part_f), (XS, low_s, part_s)):
            base = first + batch * (1 + 2 * nu)
            sent(low_mine.at[here], base)
            for c, (start, size) in enumerate(unit_cuts):
                for j in range(2):
                    sent(mine.at[j, here, span(start, size)], base + 1 + 2 * c + j)
        for c, (start, size) in enumerate(unit_cuts):
            sent(part_b.at[here, span(start, size)], XB + batch * nu + c)
    for batch in range(2):
        for c, (start, size) in enumerate(width_cuts):
            columns = pl.ds(start, size)
            sent(sum_f.at[batch, others, :, columns], RF + batch * nw + c)
            sent(sum_b.at[batch, others, :, columns], RB + batch * nw + c)


def hand_over(*refs):
    for source, target in zip(refs[:4], refs[4:]):
        target[...] = source[...]


def body(*args):
    fwd_input, saved, cotan, norm_gain, w_gate, w_up, w_down, adapt_a, adapt_b = args
    segments = lax.axis_size("segment")
    shards = lax.axis_size("hid")
    part, width = fwd_input.shape
    units = w_gate.shape[2]
    rank = adapt_a.shape[2]
    rows = part * shards
    wide = up_to(units, LANES)
    fold = (width + LANES) // 2
    nu, nw = len(cuts(units, UNIT_STEP)), len(cuts(fold, WIDTH_STEP))
    groups = 12 + 4 * (1 + 2 * nu) + 2 * nu + 4 * nw
    vmem = pltpu.VMEM
    gathered = vmem((2, shards, part, fold), B16)
    pair = vmem((2, rows, wide), B16)
    single = vmem((rows, wide), B16)
    square = vmem((rows, LANES), B16)
    term = vmem((rows, units), F32)
    block = vmem((part, fold), F32)
    pair_block = vmem((2, part, fold), F32)
    line = vmem((2, part, fold), B16)
    scratch = [
        vmem((units, width), B16), vmem((units, width), B16), vmem((units, width), B16),
        vmem((LANES, width), B16), vmem((LANES, units), B16),
        gathered, gathered, gathered, vmem((rows, width), B16),
        pair, pair, pair, pair, single, single,
        square, square, square, square, square, vmem((LANES, rows), B16), vmem((rows, LANES), F32),
        vmem((rows, LANES), F32), vmem((rows // 2, min(UNIT_STEP, units)), F32),
        vmem((rows, units), B16), vmem((rows, units), B16), vmem((rows, units), B16),
        term, term, term, vmem((2, rows, LANES), F32),
        gathered, gathered, gathered, gathered,
        vmem((rank, rows), F32), vmem((shards, rank, rows), F32),
        pair_block, pair_block, pair_block, block, block,
        line, line, vmem((2, 2, part, fold), B16), pair_block, pair_block,
        pltpu.SemaphoreType.DMA((groups,)), pltpu.SemaphoreType.DMA((groups,)),
        pltpu.SemaphoreType.DMA((3,)), pltpu.SemaphoreType.REGULAR,
    ]
    whole = pl.BlockSpec(memory_space=pltpu.VMEM)
    away = pl.BlockSpec(memory_space=pl.ANY)
    results = pl.pallas_call(
        functools.partial(kernel, (segments, shards, width, units, rank)),
        out_shape=(
            jax.ShapeDtypeStruct((1, part, width), F32),
            jax.ShapeDtypeStruct((1, part, width), F32),
            jax.ShapeDtypeStruct((1, rank, width), F32),
            jax.ShapeDtypeStruct((1, rank, units), F32),
        ),
        in_specs=[whole] * 4 + [away] * 3 + [whole] * 2,
        out_specs=(whole,) * 4,
        scratch_shapes=scratch,
        compiler_params=pltpu.CompilerParams(
            collective_id=0, has_side_effects=True, vmem_limit_bytes=56 * 1024 * 1024
        ),
    )(
        fwd_input, saved, cotan, norm_gain, jnp.swapaxes(w_gate, 1, 2), jnp.swapaxes(w_up, 1, 2),
        w_down, jnp.swapaxes(adapt_a, 1, 2), adapt_b,
    )
    fwd_out, grad_in, grad_a, grad_b = pl.pallas_call(
        hand_over,
        out_shape=tuple(jax.ShapeDtypeStruct(value.shape, value.dtype) for value in results),
        in_specs=[whole] * 4,
        out_specs=(whole,) * 4,
    )(*results)
    return fwd_out, grad_in, jnp.swapaxes(grad_a, 1, 2), grad_b


def solution(mesh):
    placed = (
        P("hid", "wid"),
        P("segment", "hid", "wid"),
        P("hid", "wid"),
        P("segment", "wid"),
        P("segment", "wid", "hid"),
        P("segment", "wid", "hid"),
        P("segment", "hid", "wid"),
        P("segment", "wid", None),
        P("segment", None, "hid"),
    )
    return jax.shard_map(
        body,
        mesh=mesh,
        in_specs=placed,
        out_specs=(
            P("segment", "hid", "wid"),
            P("segment", "hid", "wid"),
            P("segment", "wid", None),
            P("segment", None, "hid"),
        ),
        check_vma=False,
    )
```

```python
import functools
import math

import jax
import jax.numpy as jnp
from jax import lax
from jax.experimental import pallas as pl
from jax.experimental.pallas import tpu as pltpu
from jax.sharding import PartitionSpec as P

EPSILON = 1e-06
LANES = 128
UNIT_STEP = 1344
WIDTH_STEP = 768
ROOT = math.sqrt(2.0 / math.pi)
CUBE = 0.044715
MESH = pl.DeviceIdType.MESH
ACROSS = (((1,), (1,)), ((), ()))
F32 = jnp.float32
B16 = jnp.bfloat16


def cuts(total, step):
    return [(at, min(step, total - at)) for at in range(0, total, step)]


def up_to(size, step):
    return (size + step - 1) // step * step


def dot(a, b):
    return jnp.dot(a, b, preferred_element_type=F32)


def dot_across(a, b):
    return lax.dot_general(a, b, ACROSS, preferred_element_type=F32)


def two_parts(value):
    high = value.astype(B16).astype(F32)
    return high, value - high


def tail_of(value):
    high, low = two_parts(value)
    lane = lax.broadcasted_iota(jnp.int32, (value.shape[0], LANES), 1)
    return jnp.where(lane == 16, high, jnp.where(lane == 17, low, 0.0))


def turn_rows(value):
    return jnp.concatenate([value[..., 4:, :], value[..., :4, :]], axis=-2)


def swap(first, second):
    row = lax.broadcasted_iota(jnp.int32, first.shape, first.ndim - 2)
    upper = jnp.where(row < 4, first, turn_rows(second))
    lower = jnp.where(row < 4, turn_rows(first), second)
    return upper, lower


def kernel(sizes, *refs):
    segments, shards, width, units, rank = sizes
    (fwd_input, saved, cotan, gain, gate_hbm, up_hbm, down_hbm, adapt_a, adapt_b) = refs[:9]
    (fwd_out, grad_in, grad_a, grad_b) = refs[9:13]
    (
        w_gate, w_up, w_down, a_pad, b_pad,
        rows_f, rows_s, rows_b, flat,
        part_f, got_f, part_s, got_s, part_b, got_b,
        low_f, low_got_f, low_s, low_got_s, low_round, low_turned, inverse, d_low,
        tails, extra, hidden, d_gate, d_up, slope_term, active_term, inner_term, inner,
        sum_f, back_f, sum_b, back_b,
        thin, thin_got, x_in, g_in, x_saved, gain_here, gain_next,
        first_message, saved_message, next_message, y_out, g_out,
        sends, recvs, loads, turn,
    ) = refs[13:]
    section = lax.axis_index("segment")
    me = lax.axis_index("hid")
    side = lax.axis_index("wid")
    part = 8
    rows = part * shards
    full = width * 2
    unit_cuts = cuts(units, UNIT_STEP)
    fold = (width + LANES) // 2
    rest = width - fold
    width_cuts = cuts(fold, WIDTH_STEP)
    nu, nw = len(unit_cuts), len(width_cuts)
    batch_rows = rows // 2
    GF, GS, GB, THIN, XIN, GIN, GAIN = 0, 2, 4, 6, 7, 9, 11
    XF = 12
    XS = XF + 2 * (1 + 2 * nu)
    XB = XS + 2 * (1 + 2 * nu)
    RF = XB + 2 * nu
    RB = RF + 2 * nw

    def take(ref, sem):
        pltpu.make_async_copy(ref, ref, sem).wait()

    def weights(index):
        source, target = ((gate_hbm, w_gate), (up_hbm, w_up), (down_hbm, w_down))[index]
        return pltpu.make_async_copy(source.at[0], target, loads.at[index])

    for index in range(3):
        weights(index).start()

    barrier = pltpu.get_barrier_semaphore()

    def greet(who):
        pl.semaphore_signal(barrier, inc=1, device_id=who, device_id_type=MESH)

    def greet_peer(i, carry):
        greet({"hid": lax.rem(me + i, shards)})
        return carry

    lax.fori_loop(1, shards, greet_peer, 0)
    greet({"wid": 1 - side})

    @pl.when(section > 0)
    def _():
        def one(i, carry):
            greet({"segment": section - 1, "hid": lax.rem(me + i, shards)})
            return carry

        lax.fori_loop(0, shards, one, 0)

    @pl.when(section < segments - 1)
    def _():
        def one(i, carry):
            greet({"segment": section + 1, "hid": lax.rem(me + i, shards)})
            return carry

        lax.fori_loop(0, shards, one, 0)

    row8 = lax.broadcasted_iota(jnp.int32, (8, LANES), 0)

    def folded(values, tail):
        return swap(values[:, :fold], jnp.concatenate([values[:, fold:], tail], 1))

    def rounded(ref, values, tail):
        for batch, value in enumerate(folded(values, tail)):
            ref[batch] = value.astype(B16)

    nothing = jnp.zeros((part, LANES), F32)
    scales = jnp.broadcast_to(gain[...], (part, width))
    gain_here[...] = folded(scales, nothing)[0]
    saved_rows = saved[0]
    for batch, value in enumerate(folded(saved_rows, nothing)):
        x_saved[batch] = value

    def message(ref, x):
        rounded(ref, x * scales, tail_of(jnp.sum(x * x, axis=1, keepdims=True)))

    @pl.when(section == 0)
    def _():
        x = fwd_input[...]
        for batch, value in enumerate(folded(x, nothing)):
            x_in[batch] = value
        message(first_message, x)

    @pl.when(section == segments - 1)
    def _():
        g = cotan[...]
        for batch, value in enumerate(folded(g, nothing)):
            g_in[batch] = value
        rounded(first_message, g, nothing)

    message(saved_message, saved_rows)

    neighbours = jnp.where(section > 0, shards, 0) + jnp.where(section < segments - 1, shards, 0)
    pl.semaphore_wait(barrier, shards + neighbours)

    def spread(source, target, index, batch):
        pltpu.make_async_copy(
            source.at[batch], target.at[batch, me], recvs.at[index + batch]
        ).start()

        def one(i, carry):
            pltpu.make_async_remote_copy(
                src_ref=source.at[batch], dst_ref=target.at[batch, me],
                send_sem=sends.at[index + batch], recv_sem=recvs.at[index + batch],
                device_id={"hid": lax.rem(me + i, shards)}, device_id_type=MESH,
            ).start()
            return carry

        lax.fori_loop(1, shards, one, 0)

    def spread_both(source, target, index):
        for batch in range(2):
            spread(source, target, index, batch)

    def spread_to(other, source, target, index, batch):
        def one(i, carry):
            pltpu.make_async_remote_copy(
                src_ref=source.at[batch], dst_ref=target.at[batch, me],
                send_sem=sends.at[index + batch], recv_sem=recvs.at[index + batch],
                device_id={"segment": other, "hid": lax.rem(me + i, shards)}, device_id_type=MESH,
            ).start()
            return carry

        lax.fori_loop(0, shards, one, 0)

    def deliver(source, target, index, batch, columns):
        pltpu.make_async_copy(
            source.at[batch, me, :, columns], target.at[batch, me, :, columns], recvs.at[index]
        ).start()

        def one(i, carry):
            peer = lax.rem(me + i, shards)
            pltpu.make_async_remote_copy(
                src_ref=source.at[batch, peer, :, columns],
                dst_ref=target.at[batch, me, :, columns],
                send_sem=sends.at[index], recv_sem=recvs.at[index],
                device_id={"hid": peer}, device_id_type=MESH,
            ).start()
            return carry

        lax.fori_loop(1, shards, one, 0)

    def across(source, target, index):
        return pltpu.make_async_remote_copy(
            src_ref=source, dst_ref=target,
            send_sem=sends.at[index], recv_sem=recvs.at[index],
            device_id={"wid": 1 - side}, device_id_type=MESH,
        )

    def onward(other, source, target, index):
        return pltpu.make_async_remote_copy(
            src_ref=source, dst_ref=target,
            send_sem=sends.at[index], recv_sem=recvs.at[index],
            device_id={"segment": other}, device_id_type=MESH,
        )

    @pl.when(section == 0)
    def _():
        spread(first_message, rows_f, GF, 0)

    @pl.when(section == segments - 1)
    def _():
        spread_both(saved_message, rows_s, GS)

    @pl.when(section > 0)
    def _():
        onward(section - 1, gain_here, gain_next, GAIN).start()

    a_pad[...] = jnp.zeros_like(a_pad)
    a_pad[:rank, :] = adapt_a[0]
    b_pad[...] = jnp.zeros_like(b_pad)
    b_pad[:rank, :] = adapt_b[0]
    wide = part_f.shape[2]
    last = units // LANES * LANES
    if last < wide:
        for buffer in (part_f, part_s):
            for j in range(2):
                buffer[j, :, last:] = jnp.zeros((rows, wide - last), B16)
        part_b[:, last:] = jnp.zeros((rows, wide - last), B16)

    def rows_of(batch):
        return slice(batch * batch_rows, (batch + 1) * batch_rows)

    @pl.when(section == 0)
    def _():
        spread(first_message, rows_f, GF, 1)

    @pl.when(section == segments - 1)
    def _():
        spread_both(first_message, rows_b, GB)

    def flatten(source, batch):
        def one(i, carry):
            lefts, rights = [], []
            for j in range(2):
                pair = [source[batch, 4 * i + 2 * j + k].astype(F32) for k in range(2)]
                left, right = swap(pair[0], pair[1])
                lefts.append(left)
                rights.append(right)
            at_rows = pl.ds(pl.multiple_of(batch * batch_rows + i * 16, 16), 16)
            right = jnp.concatenate(rights, 0)
            flat[at_rows, :fold] = jnp.concatenate(lefts, 0).astype(B16)
            flat[at_rows, fold:] = right[:, :rest].astype(B16)
            tails[at_rows, :] = right[:, rest:]
            return carry

        lax.fori_loop(0, shards // 4, one, 0)

    def span(start, size):
        return pl.ds(start, up_to(size, LANES))

    def arrived(gathered, index, batch):
        take(gathered.at[batch], recvs.at[index + batch])
        flatten(gathered, batch)

    def project(gathered, index, mine, theirs, low_mine, low_theirs, base, batches):
        step = 1 + 2 * nu
        here = slice(batches[0] * batch_rows, (batches[-1] + 1) * batch_rows)
        for batch in batches:
            arrived(gathered, index, batch)
        low_mine[here, :] = (dot_across(flat[here, :], a_pad[...]) + tails[here, :]).astype(B16)
        for batch in batches:
            ours = rows_of(batch)
            across(low_mine.at[ours], low_theirs.at[ours], base + batch * step).start()
        for c, (start, size) in enumerate(unit_cuts):
            for j, matrix in enumerate((w_gate, w_up)):
                mine[j, here, start : start + size] = dot_across(
                    flat[here, :], matrix[start : start + size, :]
                ).astype(B16)
                for batch in batches:
                    ours = rows_of(batch)
                    across(
                        mine.at[j, ours, span(start, size)],
                        theirs.at[j, ours, span(start, size)],
                        base + batch * step + 1 + 2 * c + j,
                    ).start()

    def join_low(low_mine, low_theirs, base, batch):
        base = base + batch * (1 + 2 * nu)
        here = rows_of(batch)
        take(low_theirs.at[here], recvs.at[base])
        low = low_mine[here, :].astype(F32) + low_theirs[here, :].astype(F32)
        squares = low[:, 16:17] + low[:, 17:18]
        inv = lax.rsqrt(squares / full + EPSILON)
        inverse[here, :] = jnp.broadcast_to(inv, (batch_rows, LANES))
        lane = lax.broadcasted_iota(jnp.int32, (batch_rows, LANES), 1)
        low_round[here, :] = jnp.where(lane < rank, low * inv, 0.0).astype(B16)

    def each_block(work, batch):
        def one(i, carry):
            work(pl.ds(pl.multiple_of(batch * batch_rows + i * 16, 16), 16), i)
            return carry

        lax.fori_loop(0, batch_rows // 16, one, 0)

    def join_units(mine, theirs, base, work, batch):
        base = base + batch * (1 + 2 * nu)
        rows_here = rows_of(batch)
        for c, (start, size) in enumerate(unit_cuts):
            for j in range(2):
                take(theirs.at[j, rows_here, span(start, size)], recvs.at[base + 1 + 2 * c + j])
            extra[:, :size] = dot(low_round[rows_here, :], b_pad[:, start : start + size])
            here = slice(start, start + size)

            def block(at_rows, i):
                inv = inverse[at_rows, :1]
                gate = mine[0, at_rows, here].astype(F32) + theirs[0, at_rows, here].astype(F32)
                up = mine[1, at_rows, here].astype(F32) + theirs[1, at_rows, here].astype(F32)
                added = extra[pl.ds(pl.multiple_of(i * 16, 16), 16), :size]
                work(at_rows, here, gate * inv, up * inv + added)

            each_block(block, batch)

    def pack(target, batch, start, size, left, right):
        shape = (shards // 2, 8, size)
        even, odd = swap(left.reshape(shape), right.reshape(shape))
        for i in range(shards // 2):
            target[batch, 2 * i, :, start : start + size] = even[i].astype(B16)
            target[batch, 2 * i + 1, :, start : start + size] = odd[i].astype(B16)

    def total(received, index, batch):
        parts = []
        for c, (start, size) in enumerate(width_cuts):
            take(received.at[batch, :, :, pl.ds(start, size)], recvs.at[index + batch * nw + c])
            value = received[batch, 0, :, start : start + size].astype(F32)
            for k in range(1, shards):
                value = value + received[batch, k, :, start : start + size].astype(F32)
            parts.append(value)
        return jnp.concatenate(parts, 1)

    def send_on(other, values, tail, batch, slot, target, index):
        message_ref = next_message.at[slot]
        message_ref[batch, :, :rest] = values[:, :rest].astype(B16)
        message_ref[batch, :, rest:] = jnp.where(row8 < 4, values[:, rest:], tail).astype(B16)
        spread_to(other, message_ref, target, index, batch)

    def unfold(target, blocks):
        left, right = swap(blocks[0], blocks[1])
        target[0, :, :fold] = left
        target[0, :, fold:] = right[:, :rest]

    def forward():
        for batch in range(2):
            project(rows_f, GF, part_f, got_f, low_f, low_got_f, XF, (batch,))

        @pl.when(section == 1)
        def _():
            spread_both(saved_message, rows_s, GS)

        def work(at_rows, here, gate, up):
            bend = jnp.tanh(ROOT * (gate + CUBE * gate * gate * gate))
            hidden[at_rows, here] = (0.5 * gate * (1.0 + bend) * up).astype(B16)

        for batch in range(2):
            join_low(low_f, low_got_f, XF, batch)
            join_units(part_f, got_f, XF, work, batch)
            h = hidden[rows_of(batch), :]
            for c, (start, size) in enumerate(width_cuts):
                left = dot(h, w_down[:, start : start + size])
                real = min(size, rest - start)
                right = dot(h, w_down[:, fold + start : fold + start + real])
                if real < size:
                    right = jnp.concatenate([right, jnp.zeros((batch_rows, size - real), F32)], 1)
                pack(sum_f, batch, start, size, left, right)
                deliver(sum_f, back_f, RF + batch * nw + c, batch, pl.ds(start, size))

        @pl.when(section < segments - 1)
        def _():
            take(gain_next, recvs.at[GAIN])

        for batch in range(2):

            @pl.when(section > 0)
            def _():
                take(x_in.at[batch], recvs.at[XIN + batch])

            value = total(back_f, RF, batch)
            bottom = jnp.where(row8 < 4, value[:, rest:], 0.0)
            y = x_in[batch] + jnp.concatenate([value[:, :rest], bottom], 1)
            y_out[batch] = y

            @pl.when(section < segments - 1)
            def _():
                squares = jnp.sum(y * y, axis=1, keepdims=True)
                tail = tail_of(squares + turn_rows(squares))
                send_on(section + 1, y * gain_next[...], tail, batch, 0, rows_f, GF)
                onward(section + 1, y_out.at[batch], x_in.at[batch], XIN + batch).start()

        unfold(fwd_out, (y_out[0], y_out[1]))

    def recompute():
        @pl.when(jnp.logical_or(section == 0, section == 2))
        def _():
            pl.semaphore_wait(turn, 1)
            spread_both(saved_message, rows_s, GS)

        project(rows_s, GS, part_s, got_s, low_s, low_got_s, XS, (0, 1))

        @pl.when(section == 1)
        def _():
            pl.semaphore_signal(turn, inc=1, device_id={"segment": 0}, device_id_type=MESH)

    def join_saved():
        def work(at_rows, here, gate, up):
            bend = jnp.tanh(ROOT * (gate + CUBE * gate * gate * gate))
            active = 0.5 * gate * (1.0 + bend)
            slope = 0.5 * (1.0 + bend) + 0.5 * gate * (1.0 - bend * bend) * (
                ROOT * (1.0 + 3.0 * CUBE * gate * gate)
            )
            steep = up * slope
            slope_term[at_rows, here] = steep
            active_term[at_rows, here] = active
            inner_term[at_rows, here] = steep * gate + active * up

        for batch in range(2):
            join_low(low_s, low_got_s, XS, batch)
            join_units(part_s, got_s, XS, work, batch)
        inner[1] = inverse[...]
        low_turned[...] = low_round[...].astype(F32).T.astype(B16)

    def thin_to(i, carry):
        pltpu.make_async_remote_copy(
            src_ref=thin, dst_ref=thin_got.at[me],
            send_sem=sends.at[THIN], recv_sem=recvs.at[THIN],
            device_id={"hid": lax.rem(me + i, shards)}, device_id_type=MESH,
        ).start()
        return carry

    def adapter_gradient():
        take(thin_got, recvs.at[THIN])
        low_sum = thin_got[0]
        for k in range(1, shards):
            low_sum = low_sum + thin_got[k]
        high, low = two_parts(low_sum)
        for batch in range(2):
            flatten(rows_s, batch)
        grad_a[0] = dot(high.astype(B16), flat[...]) + dot(low.astype(B16), flat[...])

    def hand_turn():
        @pl.when(section == segments - 1)
        def _():
            pl.semaphore_signal(turn, inc=1, device_id={"segment": 2}, device_id_type=MESH)

    def backward():
        for batch in range(2):
            arrived(rows_b, GB, batch)
            if batch == 1:
                hand_turn()
            at_rows = rows_of(batch)
            for c, (start, size) in enumerate(unit_cuts):
                part_b[at_rows, start : start + size] = dot_across(
                    flat[at_rows, :], w_down[start : start + size, :]
                ).astype(B16)
                across(
                    part_b.at[at_rows, span(start, size)],
                    got_b.at[at_rows, span(start, size)],
                    XB + batch * nu + c,
                ).start()

        join_saved()
        inner[0] = jnp.zeros((rows, LANES), F32)
        for batch in range(2):
            ours = rows_of(batch)
            for c, (start, size) in enumerate(unit_cuts):
                take(got_b.at[ours, span(start, size)], recvs.at[XB + batch * nu + c])
                here = slice(start, start + size)

                def block(at_rows, i):
                    d_hid = part_b[at_rows, here].astype(F32) + got_b[at_rows, here].astype(F32)
                    d_gate[at_rows, here] = (d_hid * slope_term[at_rows, here]).astype(B16)
                    d_up[at_rows, here] = (d_hid * active_term[at_rows, here]).astype(B16)
                    inner[0, at_rows, :] += jnp.broadcast_to(
                        jnp.sum(d_hid * inner_term[at_rows, here], axis=1, keepdims=True),
                        (16, LANES),
                    )

                each_block(block, batch)
            d_low[ours, :] = dot_across(d_up[ours, :], b_pad[...])
            d_low_round = d_low[ours, :].astype(B16)
            if batch == 1:
                thin[...] = (d_low[...] * inner[1]).T[:rank]
                pltpu.make_async_copy(thin, thin_got.at[me], recvs.at[THIN]).start()
                lax.fori_loop(1, shards, thin_to, 0)
            tail = tail_of(inner[0, ours, :1])

            def product(start, size):
                here = slice(start, start + size)
                value = dot(d_gate[ours, :], w_gate[:, here])
                value = value + dot(d_up[ours, :], w_up[:, here])
                return value + dot(d_low_round, a_pad[:, here])

            for c, (start, size) in enumerate(width_cuts):
                left = product(start, size)
                real = min(size, rest - start)
                right = product(fold + start, real)
                if real < size:
                    right = jnp.concatenate([right, tail], 1)
                pack(sum_b, batch, start, size, left, right)
                deliver(sum_b, back_b, RB + batch * nw + c, batch, pl.ds(start, size))
        grad_b[0] = dot(low_turned[...], d_up[...])[:rank]

        for batch in range(2):

            @pl.when(section < segments - 1)
            def _():
                take(g_in.at[batch], recvs.at[GIN + batch])

            if batch == 1:
                adapter_gradient()
            at_row = pl.multiple_of(batch * batch_rows + me // 2 * 8, 8)
            inv = inner[1, pl.ds(at_row, 8), :]
            upper = jnp.where(lax.rem(me, 2) == 0, 0, 4)
            inv = jnp.where(row8 // 4 * 4 == upper, inv, turn_rows(inv))[:, :1]
            value = total(back_b, RB, batch)
            weight = value[:, rest + 16 : rest + 17] + value[:, rest + 17 : rest + 18]
            weight = jnp.where(row8 < 4, turn_rows(weight), weight)[:, :1]
            weight = inv * inv * weight / full
            g = g_in[batch] + inv * gain_here[...] * value - x_saved[batch] * weight
            g_out[batch] = g

            @pl.when(section > 0)
            def _():
                send_on(section - 1, g, nothing, batch, 1, rows_b, GB)
                onward(section - 1, g_out.at[batch], g_in.at[batch], GIN + batch).start()

        unfold(grad_in, (g_out[0], g_out[1]))

    for index in range(3):
        weights(index).wait()

    def moment(now, carry):
        pl.when(section == now)(forward)
        pl.when(now == jnp.where(section == 1, 1, 0))(recompute)
        pl.when(section == segments - 1 - now)(backward)
        return carry

    lax.fori_loop(0, segments, moment, 0)

    def sent(ref, index):
        take(ref, sends.at[index])

    others = pl.ds(0, shards - 1)
    for batch in range(2):

        @pl.when(section < segments - 1)
        def _():
            sent(rows_f.at[batch], GF + batch)
            sent(y_out.at[batch], XIN + batch)

        @pl.when(section > 0)
        def _():
            sent(rows_b.at[batch], GB + batch)
            sent(g_out.at[batch], GIN + batch)

        @pl.when(section == 0)
        def _():
            sent(rows_f.at[batch, others], GF + batch)

        @pl.when(section == segments - 1)
        def _():
            sent(rows_b.at[batch, others], GB + batch)

        sent(rows_s.at[batch, others], GS + batch)

    @pl.when(section > 0)
    def _():
        sent(gain_here, GAIN)

    sent(thin_got.at[others], THIN)
    for batch in range(2):
        here = rows_of(batch)
        for first, low_mine, mine in ((XF, low_f, part_f), (XS, low_s, part_s)):
            base = first + batch * (1 + 2 * nu)
            sent(low_mine.at[here], base)
            for c, (start, size) in enumerate(unit_cuts):
                for j in range(2):
                    sent(mine.at[j, here, span(start, size)], base + 1 + 2 * c + j)
        for c, (start, size) in enumerate(unit_cuts):
            sent(part_b.at[here, span(start, size)], XB + batch * nu + c)
    for batch in range(2):
        for c, (start, size) in enumerate(width_cuts):
            columns = pl.ds(start, size)
            sent(sum_f.at[batch, others, :, columns], RF + batch * nw + c)
            sent(sum_b.at[batch, others, :, columns], RB + batch * nw + c)


def hand_over(*refs):
    for source, target in zip(refs[:4], refs[4:]):
        target[...] = source[...]


def body(*args):
    fwd_input, saved, cotan, norm_gain, w_gate, w_up, w_down, adapt_a, adapt_b = args
    segments = lax.axis_size("segment")
    shards = lax.axis_size("hid")
    part, width = fwd_input.shape
    units = w_gate.shape[2]
    rank = adapt_a.shape[2]
    rows = part * shards
    wide = up_to(units, LANES)
    fold = (width + LANES) // 2
    nu, nw = len(cuts(units, UNIT_STEP)), len(cuts(fold, WIDTH_STEP))
    groups = 12 + 4 * (1 + 2 * nu) + 2 * nu + 4 * nw
    vmem = pltpu.VMEM
    gathered = vmem((2, shards, part, fold), B16)
    pair = vmem((2, rows, wide), B16)
    single = vmem((rows, wide), B16)
    square = vmem((rows, LANES), B16)
    term = vmem((rows, units), F32)
    block = vmem((part, fold), F32)
    pair_block = vmem((2, part, fold), F32)
    line = vmem((2, part, fold), B16)
    scratch = [
        vmem((units, width), B16), vmem((units, width), B16), vmem((units, width), B16),
        vmem((LANES, width), B16), vmem((LANES, units), B16),
        gathered, gathered, gathered, vmem((rows, width), B16),
        pair, pair, pair, pair, single, single,
        square, square, square, square, square, vmem((LANES, rows), B16), vmem((rows, LANES), F32), vmem((rows, LANES), F32),
        vmem((rows, LANES), F32), vmem((rows // 2, min(UNIT_STEP, units)), F32),
        vmem((rows, units), B16), vmem((rows, units), B16), vmem((rows, units), B16),
        term, term, term, vmem((2, rows, LANES), F32),
        gathered, gathered, gathered, gathered,
        vmem((rank, rows), F32), vmem((shards, rank, rows), F32),
        pair_block, pair_block, pair_block, block, block,
        line, line, vmem((2, 2, part, fold), B16), pair_block, pair_block,
        pltpu.SemaphoreType.DMA((groups,)), pltpu.SemaphoreType.DMA((groups,)),
        pltpu.SemaphoreType.DMA((3,)), pltpu.SemaphoreType.REGULAR,
    ]
    whole = pl.BlockSpec(memory_space=pltpu.VMEM)
    away = pl.BlockSpec(memory_space=pl.ANY)
    results = pl.pallas_call(
        functools.partial(kernel, (segments, shards, width, units, rank)),
        out_shape=(
            jax.ShapeDtypeStruct((1, part, width), F32),
            jax.ShapeDtypeStruct((1, part, width), F32),
            jax.ShapeDtypeStruct((1, rank, width), F32),
            jax.ShapeDtypeStruct((1, rank, units), F32),
        ),
        in_specs=[whole] * 4 + [away] * 3 + [whole] * 2,
        out_specs=(whole,) * 4,
        scratch_shapes=scratch,
        compiler_params=pltpu.CompilerParams(
            collective_id=0, has_side_effects=True, vmem_limit_bytes=56 * 1024 * 1024
        ),
    )(
        fwd_input, saved, cotan, norm_gain, jnp.swapaxes(w_gate, 1, 2), jnp.swapaxes(w_up, 1, 2),
        w_down, jnp.swapaxes(adapt_a, 1, 2), adapt_b,
    )
    fwd_out, grad_in, grad_a, grad_b = pl.pallas_call(
        hand_over,
        out_shape=tuple(jax.ShapeDtypeStruct(value.shape, value.dtype) for value in results),
        in_specs=[whole] * 4,
        out_specs=(whole,) * 4,
    )(*results)
    return fwd_out, grad_in, jnp.swapaxes(grad_a, 1, 2), grad_b


def solution(mesh):
    placed = (
        P("hid", "wid"),
        P("segment", "hid", "wid"),
        P("hid", "wid"),
        P("segment", "wid"),
        P("segment", "wid", "hid"),
        P("segment", "wid", "hid"),
        P("segment", "hid", "wid"),
        P("segment", "wid", None),
        P("segment", None, "hid"),
    )
    return jax.shard_map(
        body,
        mesh=mesh,
        in_specs=placed,
        out_specs=(
            P("segment", "hid", "wid"),
            P("segment", "hid", "wid"),
            P("segment", "wid", None),
            P("segment", None, "hid"),
        ),
        check_vma=False,
    )
```

```python
import functools
import math

import jax
import jax.numpy as jnp
from jax import lax
from jax.experimental import pallas as pl
from jax.experimental.pallas import tpu as pltpu
from jax.sharding import PartitionSpec as P

EPSILON = 1e-06
LANES = 128
UNIT_STEP = 1344
WIDTH_STEP = 768
ROOT = math.sqrt(2.0 / math.pi)
CUBE = 0.044715
MESH = pl.DeviceIdType.MESH
ACROSS = (((1,), (1,)), ((), ()))
F32 = jnp.float32
B16 = jnp.bfloat16


def cuts(total, step):
    return [(at, min(step, total - at)) for at in range(0, total, step)]


def up_to(size, step):
    return (size + step - 1) // step * step


def dot(a, b):
    return jnp.dot(a, b, preferred_element_type=F32)


def dot_across(a, b):
    return lax.dot_general(a, b, ACROSS, preferred_element_type=F32)


def two_parts(value):
    high = value.astype(B16).astype(F32)
    return high, value - high


def tail_of(value):
    high, low = two_parts(value)
    lane = lax.broadcasted_iota(jnp.int32, (value.shape[0], LANES), 1)
    return jnp.where(lane == 16, high, jnp.where(lane == 17, low, 0.0))


def turn_rows(value):
    return jnp.concatenate([value[..., 4:, :], value[..., :4, :]], axis=-2)


def swap(first, second):
    row = lax.broadcasted_iota(jnp.int32, first.shape, first.ndim - 2)
    upper = jnp.where(row < 4, first, turn_rows(second))
    lower = jnp.where(row < 4, turn_rows(first), second)
    return upper, lower


def kernel(sizes, *refs):
    segments, shards, width, units, rank = sizes
    (fwd_input, saved, cotan, gain, gate_hbm, up_hbm, down_hbm, adapt_a, adapt_b) = refs[:9]
    (fwd_out, grad_in, grad_a, grad_b) = refs[9:13]
    (
        w_gate, w_up, w_down, a_pad, b_pad,
        rows_f, rows_s, rows_b, flat,
        part_f, got_f, part_s, got_s, part_b, got_b,
        low_f, low_got_f, low_s, low_got_s, low_round, low_turned, inverse, d_low,
        tails, extra, hidden, d_gate, d_up, slope_term, active_term, inner_term, inner,
        sum_f, back_f, sum_b, back_b,
        thin, thin_got, x_in, g_in, x_saved, gain_here, gain_next,
        first_message, saved_message, next_message, y_out, g_out,
        sends, recvs, loads, turn,
    ) = refs[13:]
    section = lax.axis_index("segment")
    me = lax.axis_index("hid")
    side = lax.axis_index("wid")
    part = 8
    rows = part * shards
    full = width * 2
    unit_cuts = cuts(units, UNIT_STEP)
    fold = (width + LANES) // 2
    rest = width - fold
    width_cuts = cuts(fold, WIDTH_STEP)
    nu, nw = len(unit_cuts), len(width_cuts)
    batch_rows = rows // 2
    GF, GS, GB, THIN, XIN, GIN, GAIN = 0, 2, 4, 6, 7, 9, 11
    XF = 12
    XS = XF + 2 * (1 + 2 * nu)
    XB = XS + 2 * (1 + 2 * nu)
    RF = XB + 2 * nu
    RB = RF + 2 * nw

    def take(ref, sem):
        pltpu.make_async_copy(ref, ref, sem).wait()

    def weights(index):
        source, target = ((gate_hbm, w_gate), (up_hbm, w_up), (down_hbm, w_down))[index]
        return pltpu.make_async_copy(source.at[0], target, loads.at[index])

    for index in range(2):
        weights(index).start()

    barrier = pltpu.get_barrier_semaphore()

    def greet(who):
        pl.semaphore_signal(barrier, inc=1, device_id=who, device_id_type=MESH)

    def greet_peer(i, carry):
        greet({"hid": lax.rem(me + i, shards)})
        return carry

    lax.fori_loop(1, shards, greet_peer, 0)
    greet({"wid": 1 - side})

    @pl.when(section > 0)
    def _():
        def one(i, carry):
            greet({"segment": section - 1, "hid": lax.rem(me + i, shards)})
            return carry

        lax.fori_loop(0, shards, one, 0)

    @pl.when(section < segments - 1)
    def _():
        def one(i, carry):
            greet({"segment": section + 1, "hid": lax.rem(me + i, shards)})
            return carry

        lax.fori_loop(0, shards, one, 0)

    row8 = lax.broadcasted_iota(jnp.int32, (8, LANES), 0)

    def folded(values, tail):
        return swap(values[:, :fold], jnp.concatenate([values[:, fold:], tail], 1))

    def rounded(ref, values, tail):
        for batch, value in enumerate(folded(values, tail)):
            ref[batch] = value.astype(B16)

    nothing = jnp.zeros((part, LANES), F32)
    scales = jnp.broadcast_to(gain[...], (part, width))
    gain_here[...] = folded(scales, nothing)[0]
    saved_rows = saved[0]
    for batch, value in enumerate(folded(saved_rows, nothing)):
        x_saved[batch] = value

    def message(ref, x):
        rounded(ref, x * scales, tail_of(jnp.sum(x * x, axis=1, keepdims=True)))

    @pl.when(section == 0)
    def _():
        x = fwd_input[...]
        for batch, value in enumerate(folded(x, nothing)):
            x_in[batch] = value
        message(first_message, x)

    @pl.when(section == segments - 1)
    def _():
        g = cotan[...]
        for batch, value in enumerate(folded(g, nothing)):
            g_in[batch] = value
        rounded(first_message, g, nothing)

    message(saved_message, saved_rows)

    neighbours = jnp.where(section > 0, shards, 0) + jnp.where(section < segments - 1, shards, 0)
    pl.semaphore_wait(barrier, shards + neighbours)

    def spread(source, target, index, batch):
        pltpu.make_async_copy(
            source.at[batch], target.at[batch, me], recvs.at[index + batch]
        ).start()

        def one(i, carry):
            pltpu.make_async_remote_copy(
                src_ref=source.at[batch], dst_ref=target.at[batch, me],
                send_sem=sends.at[index + batch], recv_sem=recvs.at[index + batch],
                device_id={"hid": lax.rem(me + i, shards)}, device_id_type=MESH,
            ).start()
            return carry

        lax.fori_loop(1, shards, one, 0)

    def spread_both(source, target, index):
        for batch in range(2):
            spread(source, target, index, batch)

    def spread_to(other, source, target, index, batch):
        def one(i, carry):
            pltpu.make_async_remote_copy(
                src_ref=source.at[batch], dst_ref=target.at[batch, me],
                send_sem=sends.at[index + batch], recv_sem=recvs.at[index + batch],
                device_id={"segment": other, "hid": lax.rem(me + i, shards)}, device_id_type=MESH,
            ).start()
            return carry

        lax.fori_loop(0, shards, one, 0)

    def deliver(source, target, index, batch, columns):
        pltpu.make_async_copy(
            source.at[batch, me, :, columns], target.at[batch, me, :, columns], recvs.at[index]
        ).start()

        def one(i, carry):
            peer = lax.rem(me + i, shards)
            pltpu.make_async_remote_copy(
                src_ref=source.at[batch, peer, :, columns],
                dst_ref=target.at[batch, me, :, columns],
                send_sem=sends.at[index], recv_sem=recvs.at[index],
                device_id={"hid": peer}, device_id_type=MESH,
            ).start()
            return carry

        lax.fori_loop(1, shards, one, 0)

    def across(source, target, index):
        return pltpu.make_async_remote_copy(
            src_ref=source, dst_ref=target,
            send_sem=sends.at[index], recv_sem=recvs.at[index],
            device_id={"wid": 1 - side}, device_id_type=MESH,
        )

    def onward(other, source, target, index):
        return pltpu.make_async_remote_copy(
            src_ref=source, dst_ref=target,
            send_sem=sends.at[index], recv_sem=recvs.at[index],
            device_id={"segment": other}, device_id_type=MESH,
        )

    @pl.when(section == 0)
    def _():
        spread(first_message, rows_f, GF, 0)

    @pl.when(section == segments - 1)
    def _():
        spread_both(saved_message, rows_s, GS)

    @pl.when(section > 0)
    def _():
        onward(section - 1, gain_here, gain_next, GAIN).start()

    weights(2).start()

    a_pad[...] = jnp.zeros_like(a_pad)
    a_pad[:rank, :] = adapt_a[0]
    b_pad[...] = jnp.zeros_like(b_pad)
    b_pad[:rank, :] = adapt_b[0]
    wide = part_f.shape[2]
    last = units // LANES * LANES
    if last < wide:
        for buffer in (part_f, part_s):
            for j in range(2):
                buffer[j, :, last:] = jnp.zeros((rows, wide - last), B16)
        part_b[:, last:] = jnp.zeros((rows, wide - last), B16)

    def rows_of(batch):
        return slice(batch * batch_rows, (batch + 1) * batch_rows)

    @pl.when(section == 0)
    def _():
        spread(first_message, rows_f, GF, 1)

    @pl.when(section == segments - 1)
    def _():
        spread_both(first_message, rows_b, GB)

    def flatten(source, batch):
        def one(i, carry):
            lefts, rights = [], []
            for j in range(2):
                pair = [source[batch, 4 * i + 2 * j + k].astype(F32) for k in range(2)]
                left, right = swap(pair[0], pair[1])
                lefts.append(left)
                rights.append(right)
            at_rows = pl.ds(pl.multiple_of(batch * batch_rows + i * 16, 16), 16)
            right = jnp.concatenate(rights, 0)
            flat[at_rows, :fold] = jnp.concatenate(lefts, 0).astype(B16)
            flat[at_rows, fold:] = right[:, :rest].astype(B16)
            tails[at_rows, :] = right[:, rest:]
            return carry

        lax.fori_loop(0, shards // 4, one, 0)

    def span(start, size):
        return pl.ds(start, up_to(size, LANES))

    def arrived(gathered, index, batch):
        take(gathered.at[batch], recvs.at[index + batch])
        flatten(gathered, batch)

    def project(gathered, index, mine, theirs, low_mine, low_theirs, base, batches):
        step = 1 + 2 * nu
        here = slice(batches[0] * batch_rows, (batches[-1] + 1) * batch_rows)
        for batch in batches:
            arrived(gathered, index, batch)
        low_mine[here, :] = (dot_across(flat[here, :], a_pad[...]) + tails[here, :]).astype(B16)
        for batch in batches:
            ours = rows_of(batch)
            across(low_mine.at[ours], low_theirs.at[ours], base + batch * step).start()
        for c, (start, size) in enumerate(unit_cuts):
            for j, matrix in enumerate((w_gate, w_up)):
                mine[j, here, start : start + size] = dot_across(
                    flat[here, :], matrix[start : start + size, :]
                ).astype(B16)
                for batch in batches:
                    ours = rows_of(batch)
                    across(
                        mine.at[j, ours, span(start, size)],
                        theirs.at[j, ours, span(start, size)],
                        base + batch * step + 1 + 2 * c + j,
                    ).start()

    def join_low(low_mine, low_theirs, base, batch):
        base = base + batch * (1 + 2 * nu)
        here = rows_of(batch)
        take(low_theirs.at[here], recvs.at[base])
        low = low_mine[here, :].astype(F32) + low_theirs[here, :].astype(F32)
        squares = low[:, 16:17] + low[:, 17:18]
        inv = lax.rsqrt(squares / full + EPSILON)
        inverse[here, :] = jnp.broadcast_to(inv, (batch_rows, LANES))
        lane = lax.broadcasted_iota(jnp.int32, (batch_rows, LANES), 1)
        low_round[here, :] = jnp.where(lane < rank, low * inv, 0.0).astype(B16)

    def each_block(work, batch):
        def one(i, carry):
            work(pl.ds(pl.multiple_of(batch * batch_rows + i * 16, 16), 16), i)
            return carry

        lax.fori_loop(0, batch_rows // 16, one, 0)

    def join_units(mine, theirs, base, work, batch):
        base = base + batch * (1 + 2 * nu)
        rows_here = rows_of(batch)
        for c, (start, size) in enumerate(unit_cuts):
            for j in range(2):
                take(theirs.at[j, rows_here, span(start, size)], recvs.at[base + 1 + 2 * c + j])
            extra[:, :size] = dot(low_round[rows_here, :], b_pad[:, start : start + size])
            here = slice(start, start + size)

            def block(at_rows, i):
                inv = inverse[at_rows, :1]
                gate = mine[0, at_rows, here].astype(F32) + theirs[0, at_rows, here].astype(F32)
                up = mine[1, at_rows, here].astype(F32) + theirs[1, at_rows, here].astype(F32)
                added = extra[pl.ds(pl.multiple_of(i * 16, 16), 16), :size]
                work(at_rows, here, gate * inv, up * inv + added)

            each_block(block, batch)

    def pack(target, batch, start, size, left, right):
        shape = (shards // 2, 8, size)
        even, odd = swap(left.reshape(shape), right.reshape(shape))
        for i in range(shards // 2):
            target[batch, 2 * i, :, start : start + size] = even[i].astype(B16)
            target[batch, 2 * i + 1, :, start : start + size] = odd[i].astype(B16)

    def total(received, index, batch):
        parts = []
        for c, (start, size) in enumerate(width_cuts):
            take(received.at[batch, :, :, pl.ds(start, size)], recvs.at[index + batch * nw + c])
            value = received[batch, 0, :, start : start + size].astype(F32)
            for k in range(1, shards):
                value = value + received[batch, k, :, start : start + size].astype(F32)
            parts.append(value)
        return jnp.concatenate(parts, 1)

    def send_on(other, values, tail, batch, slot, target, index):
        message_ref = next_message.at[slot]
        message_ref[batch, :, :rest] = values[:, :rest].astype(B16)
        message_ref[batch, :, rest:] = jnp.where(row8 < 4, values[:, rest:], tail).astype(B16)
        spread_to(other, message_ref, target, index, batch)

    def unfold(target, blocks):
        left, right = swap(blocks[0], blocks[1])
        target[0, :, :fold] = left
        target[0, :, fold:] = right[:, :rest]

    def forward():
        for batch in range(2):
            project(rows_f, GF, part_f, got_f, low_f, low_got_f, XF, (batch,))

        @pl.when(section <= 1)
        def _():
            weights(2).wait()

        @pl.when(section == 1)
        def _():
            spread_both(saved_message, rows_s, GS)

        def work(at_rows, here, gate, up):
            bend = jnp.tanh(ROOT * (gate + CUBE * gate * gate * gate))
            hidden[at_rows, here] = (0.5 * gate * (1.0 + bend) * up).astype(B16)

        for batch in range(2):
            join_low(low_f, low_got_f, XF, batch)
            join_units(part_f, got_f, XF, work, batch)
            h = hidden[rows_of(batch), :]
            for c, (start, size) in enumerate(width_cuts):
                left = dot(h, w_down[:, start : start + size])
                real = min(size, rest - start)
                right = dot(h, w_down[:, fold + start : fold + start + real])
                if real < size:
                    right = jnp.concatenate([right, jnp.zeros((batch_rows, size - real), F32)], 1)
                pack(sum_f, batch, start, size, left, right)
                deliver(sum_f, back_f, RF + batch * nw + c, batch, pl.ds(start, size))

        @pl.when(section < segments - 1)
        def _():
            take(gain_next, recvs.at[GAIN])

        for batch in range(2):

            @pl.when(section > 0)
            def _():
                take(x_in.at[batch], recvs.at[XIN + batch])

            value = total(back_f, RF, batch)
            bottom = jnp.where(row8 < 4, value[:, rest:], 0.0)
            y = x_in[batch] + jnp.concatenate([value[:, :rest], bottom], 1)
            y_out[batch] = y

            @pl.when(section < segments - 1)
            def _():
                squares = jnp.sum(y * y, axis=1, keepdims=True)
                tail = tail_of(squares + turn_rows(squares))
                send_on(section + 1, y * gain_next[...], tail, batch, 0, rows_f, GF)
                onward(section + 1, y_out.at[batch], x_in.at[batch], XIN + batch).start()

        unfold(fwd_out, (y_out[0], y_out[1]))

    def recompute():
        @pl.when(jnp.logical_or(section == 0, section == 2))
        def _():
            pl.semaphore_wait(turn, 1)
            spread_both(saved_message, rows_s, GS)

        project(rows_s, GS, part_s, got_s, low_s, low_got_s, XS, (0, 1))

        @pl.when(section >= 2)
        def _():
            weights(2).wait()

        @pl.when(section == 1)
        def _():
            pl.semaphore_signal(turn, inc=1, device_id={"segment": 0}, device_id_type=MESH)

    def join_saved():
        def work(at_rows, here, gate, up):
            bend = jnp.tanh(ROOT * (gate + CUBE * gate * gate * gate))
            active = 0.5 * gate * (1.0 + bend)
            slope = 0.5 * (1.0 + bend) + 0.5 * gate * (1.0 - bend * bend) * (
                ROOT * (1.0 + 3.0 * CUBE * gate * gate)
            )
            steep = up * slope
            slope_term[at_rows, here] = steep
            active_term[at_rows, here] = active
            inner_term[at_rows, here] = steep * gate + active * up

        for batch in range(2):
            join_low(low_s, low_got_s, XS, batch)
            join_units(part_s, got_s, XS, work, batch)
        inner[1] = inverse[...]
        low_turned[...] = low_round[...].astype(F32).T.astype(B16)

    def thin_to(i, carry):
        pltpu.make_async_remote_copy(
            src_ref=thin, dst_ref=thin_got.at[me],
            send_sem=sends.at[THIN], recv_sem=recvs.at[THIN],
            device_id={"hid": lax.rem(me + i, shards)}, device_id_type=MESH,
        ).start()
        return carry

    def adapter_gradient():
        take(thin_got, recvs.at[THIN])
        low_sum = thin_got[0]
        for k in range(1, shards):
            low_sum = low_sum + thin_got[k]
        high, low = two_parts(low_sum)
        for batch in range(2):
            flatten(rows_s, batch)
        grad_a[0] = dot(high.astype(B16), flat[...]) + dot(low.astype(B16), flat[...])

    def hand_turn():
        @pl.when(section == segments - 1)
        def _():
            pl.semaphore_signal(turn, inc=1, device_id={"segment": 2}, device_id_type=MESH)

    def backward():
        for batch in range(2):
            arrived(rows_b, GB, batch)
            if batch == 1:
                hand_turn()
            at_rows = rows_of(batch)
            for c, (start, size) in enumerate(unit_cuts):
                part_b[at_rows, start : start + size] = dot_across(
                    flat[at_rows, :], w_down[start : start + size, :]
                ).astype(B16)
                across(
                    part_b.at[at_rows, span(start, size)],
                    got_b.at[at_rows, span(start, size)],
                    XB + batch * nu + c,
                ).start()

        join_saved()
        inner[0] = jnp.zeros((rows, LANES), F32)
        for batch in range(2):
            ours = rows_of(batch)
            for c, (start, size) in enumerate(unit_cuts):
                take(got_b.at[ours, span(start, size)], recvs.at[XB + batch * nu + c])
                here = slice(start, start + size)

                def block(at_rows, i):
                    d_hid = part_b[at_rows, here].astype(F32) + got_b[at_rows, here].astype(F32)
                    d_gate[at_rows, here] = (d_hid * slope_term[at_rows, here]).astype(B16)
                    d_up[at_rows, here] = (d_hid * active_term[at_rows, here]).astype(B16)
                    inner[0, at_rows, :] += jnp.broadcast_to(
                        jnp.sum(d_hid * inner_term[at_rows, here], axis=1, keepdims=True),
                        (16, LANES),
                    )

                each_block(block, batch)
            d_low[ours, :] = dot_across(d_up[ours, :], b_pad[...])
            d_low_round = d_low[ours, :].astype(B16)
            if batch == 1:
                thin[...] = (d_low[...] * inner[1]).T[:rank]
                pltpu.make_async_copy(thin, thin_got.at[me], recvs.at[THIN]).start()
                lax.fori_loop(1, shards, thin_to, 0)
            tail = tail_of(inner[0, ours, :1])

            def product(start, size):
                here = slice(start, start + size)
                value = dot(d_gate[ours, :], w_gate[:, here])
                value = value + dot(d_up[ours, :], w_up[:, here])
                return value + dot(d_low_round, a_pad[:, here])

            for c, (start, size) in enumerate(width_cuts):
                left = product(start, size)
                real = min(size, rest - start)
                right = product(fold + start, real)
                if real < size:
                    right = jnp.concatenate([right, tail], 1)
                pack(sum_b, batch, start, size, left, right)
                deliver(sum_b, back_b, RB + batch * nw + c, batch, pl.ds(start, size))
        grad_b[0] = dot(low_turned[...], d_up[...])[:rank]

        for batch in range(2):

            @pl.when(section < segments - 1)
            def _():
                take(g_in.at[batch], recvs.at[GIN + batch])

            if batch == 1:
                adapter_gradient()
            at_row = pl.multiple_of(batch * batch_rows + me // 2 * 8, 8)
            inv = inner[1, pl.ds(at_row, 8), :]
            upper = jnp.where(lax.rem(me, 2) == 0, 0, 4)
            inv = jnp.where(row8 // 4 * 4 == upper, inv, turn_rows(inv))[:, :1]
            value = total(back_b, RB, batch)
            weight = value[:, rest + 16 : rest + 17] + value[:, rest + 17 : rest + 18]
            weight = jnp.where(row8 < 4, turn_rows(weight), weight)[:, :1]
            weight = inv * inv * weight / full
            g = g_in[batch] + inv * gain_here[...] * value - x_saved[batch] * weight
            g_out[batch] = g

            @pl.when(section > 0)
            def _():
                send_on(section - 1, g, nothing, batch, 1, rows_b, GB)
                onward(section - 1, g_out.at[batch], g_in.at[batch], GIN + batch).start()

        unfold(grad_in, (g_out[0], g_out[1]))

    for index in range(2):
        weights(index).wait()

    def moment(now, carry):
        pl.when(section == now)(forward)
        pl.when(now == jnp.where(section == 1, 1, 0))(recompute)
        pl.when(section == segments - 1 - now)(backward)
        return carry

    lax.fori_loop(0, segments, moment, 0)

    def sent(ref, index):
        take(ref, sends.at[index])

    others = pl.ds(0, shards - 1)
    for batch in range(2):

        @pl.when(section < segments - 1)
        def _():
            sent(rows_f.at[batch], GF + batch)
            sent(y_out.at[batch], XIN + batch)

        @pl.when(section > 0)
        def _():
            sent(rows_b.at[batch], GB + batch)
            sent(g_out.at[batch], GIN + batch)

        @pl.when(section == 0)
        def _():
            sent(rows_f.at[batch, others], GF + batch)

        @pl.when(section == segments - 1)
        def _():
            sent(rows_b.at[batch, others], GB + batch)

        sent(rows_s.at[batch, others], GS + batch)

    @pl.when(section > 0)
    def _():
        sent(gain_here, GAIN)

    sent(thin_got.at[others], THIN)
    for batch in range(2):
        here = rows_of(batch)
        for first, low_mine, mine in ((XF, low_f, part_f), (XS, low_s, part_s)):
            base = first + batch * (1 + 2 * nu)
            sent(low_mine.at[here], base)
            for c, (start, size) in enumerate(unit_cuts):
                for j in range(2):
                    sent(mine.at[j, here, span(start, size)], base + 1 + 2 * c + j)
        for c, (start, size) in enumerate(unit_cuts):
            sent(part_b.at[here, span(start, size)], XB + batch * nu + c)
    for batch in range(2):
        for c, (start, size) in enumerate(width_cuts):
            columns = pl.ds(start, size)
            sent(sum_f.at[batch, others, :, columns], RF + batch * nw + c)
            sent(sum_b.at[batch, others, :, columns], RB + batch * nw + c)


def hand_over(*refs):
    for source, target in zip(refs[:4], refs[4:]):
        target[...] = source[...]


def body(*args):
    fwd_input, saved, cotan, norm_gain, w_gate, w_up, w_down, adapt_a, adapt_b = args
    segments = lax.axis_size("segment")
    shards = lax.axis_size("hid")
    part, width = fwd_input.shape
    units = w_gate.shape[2]
    rank = adapt_a.shape[2]
    rows = part * shards
    wide = up_to(units, LANES)
    fold = (width + LANES) // 2
    nu, nw = len(cuts(units, UNIT_STEP)), len(cuts(fold, WIDTH_STEP))
    groups = 12 + 4 * (1 + 2 * nu) + 2 * nu + 4 * nw
    vmem = pltpu.VMEM
    gathered = vmem((2, shards, part, fold), B16)
    pair = vmem((2, rows, wide), B16)
    single = vmem((rows, wide), B16)
    square = vmem((rows, LANES), B16)
    term = vmem((rows, units), F32)
    block = vmem((part, fold), F32)
    pair_block = vmem((2, part, fold), F32)
    line = vmem((2, part, fold), B16)
    scratch = [
        vmem((units, width), B16), vmem((units, width), B16), vmem((units, width), B16),
        vmem((LANES, width), B16), vmem((LANES, units), B16),
        gathered, gathered, gathered, vmem((rows, width), B16),
        pair, pair, pair, pair, single, single,
        square, square, square, square, square, vmem((LANES, rows), B16), vmem((rows, LANES), F32), vmem((rows, LANES), F32),
        vmem((rows, LANES), F32), vmem((rows // 2, min(UNIT_STEP, units)), F32),
        vmem((rows, units), B16), vmem((rows, units), B16), vmem((rows, units), B16),
        term, term, term, vmem((2, rows, LANES), F32),
        gathered, gathered, gathered, gathered,
        vmem((rank, rows), F32), vmem((shards, rank, rows), F32),
        pair_block, pair_block, pair_block, block, block,
        line, line, vmem((2, 2, part, fold), B16), pair_block, pair_block,
        pltpu.SemaphoreType.DMA((groups,)), pltpu.SemaphoreType.DMA((groups,)),
        pltpu.SemaphoreType.DMA((3,)), pltpu.SemaphoreType.REGULAR,
    ]
    whole = pl.BlockSpec(memory_space=pltpu.VMEM)
    away = pl.BlockSpec(memory_space=pl.ANY)
    results = pl.pallas_call(
        functools.partial(kernel, (segments, shards, width, units, rank)),
        out_shape=(
            jax.ShapeDtypeStruct((1, part, width), F32),
            jax.ShapeDtypeStruct((1, part, width), F32),
            jax.ShapeDtypeStruct((1, rank, width), F32),
            jax.ShapeDtypeStruct((1, rank, units), F32),
        ),
        in_specs=[whole] * 4 + [away] * 3 + [whole] * 2,
        out_specs=(whole,) * 4,
        scratch_shapes=scratch,
        compiler_params=pltpu.CompilerParams(
            collective_id=0, has_side_effects=True, vmem_limit_bytes=56 * 1024 * 1024
        ),
    )(
        fwd_input, saved, cotan, norm_gain, jnp.swapaxes(w_gate, 1, 2), jnp.swapaxes(w_up, 1, 2),
        w_down, jnp.swapaxes(adapt_a, 1, 2), adapt_b,
    )
    fwd_out, grad_in, grad_a, grad_b = pl.pallas_call(
        hand_over,
        out_shape=tuple(jax.ShapeDtypeStruct(value.shape, value.dtype) for value in results),
        in_specs=[whole] * 4,
        out_specs=(whole,) * 4,
    )(*results)
    return fwd_out, grad_in, jnp.swapaxes(grad_a, 1, 2), grad_b


def solution(mesh):
    placed = (
        P("hid", "wid"),
        P("segment", "hid", "wid"),
        P("hid", "wid"),
        P("segment", "wid"),
        P("segment", "wid", "hid"),
        P("segment", "wid", "hid"),
        P("segment", "hid", "wid"),
        P("segment", "wid", None),
        P("segment", None, "hid"),
    )
    return jax.shard_map(
        body,
        mesh=mesh,
        in_specs=placed,
        out_specs=(
            P("segment", "hid", "wid"),
            P("segment", "hid", "wid"),
            P("segment", "wid", None),
            P("segment", None, "hid"),
        ),
        check_vma=False,
    )
```
